128 devices in a mesh: row: 8 (over x_lo, y), col: 16 (over z, x_hi, core).
Axes of the slice: x: 4 (x_hi: 2, x_lo: 2; x = x_hi * 2 + x_lo), y: 4, z: 4, core: 2. Of those that a mesh axis runs over, the one named last changes fastest.
Arguments:
- activations: bfloat16 [1280, 28672], P('col', 'row'), may hold values from -6 to 6
- gradients: bfloat16 [1280, 8192], P('row', 'col'), may hold values from -0.0014953613 to 0.0014953613
- basis_in: bfloat16 [28672, 28672], P('row', 'col'), may hold values from -0.03125 to 0.03125
- basis_out: bfloat16 [8192, 8192], P('col', 'row'), may hold values from -0.0625 to 0.0625
- eigen_damped: float32 [8192, 28672], P('row', 'col'), may hold values from 0.1 to 4
- pair_ids: int32 [1024], replicated, may hold values from 0 to 3, never falling along the last dimension, each value on 1 to 384 neighbouring positions
Outputs:
- scores: float32 [4, 64], replicated
The draws below stay inside these ranges and needn't reach their ends.
Inputs may be any that keep to these rules, and one draw needn't show every extreme that they name: `pair_ids`: ids never fall; every pair has 1 to 384 tokens, and some pair has exactly 384.
All inputs are finite; a program needn't handle non-finite values.
Results may differ from the reference program's by a relative error of at most 0.0046.
Values may be sent and summed in bfloat16 or wider, within the bound.
A program may use at most 128 MiB of HBM per device.

```python
import math
import jax
import jax.numpy as jnp
import numpy as np
from jax import lax

D = 8192
F = 28672
PAIRS = 4
TOKENS = 1024
QUERIES = 64
QLEN = 4
MOST = 384
ALL_TOK = 1280


def steps_of(own_key, shape, shards, least, largest):
    def one(dim, blocks):
        draws = jax.random.uniform(jax.random.fold_in(jax.random.fold_in(own_key, 6), dim), (blocks,), jnp.float32, least / len(shards), largest / len(shards))
        return jnp.repeat(jnp.exp(draws), shape[dim] // blocks).reshape((-1,) + (1,) * (len(shape) - dim - 1))

    gain = one(*shards[0])
    for cut in shards[1:]:
        gain = gain * one(*cut)
    return gain


def profile(count, total, bound, skew):
    weights = [(1 << 20) // math.isqrt(rank ** skew) + 1 for rank in range(2, count + 1)]
    surplus, given = total - bound - (count - 1), [1] * (count - 1)
    while surplus > 0:
        free = [i for i in range(count - 1) if given[i] < bound]
        mass, budget = sum([weights[i] for i in free]), surplus
        for i in free:
            more = min(bound - given[i], max(1, budget * weights[i] // mass), surplus)
            given[i] = given[i] + more
            surplus = surplus - more
    return np.array([bound] + given)


def uneven_parts(rng, number_of, total, most, skew):
    if number_of == 2:
        one = jax.random.randint(rng, (), max(1, total - most), min(most, total - 1) + 1)
        return jnp.stack([one, total - one])
    lengths = jnp.asarray(profile(number_of, total, most, skew), jnp.int32)
    pairs = (number_of - 1) // 2
    donor, taker = lengths[1:1 + 2 * pairs:2], lengths[2:2 + 2 * pairs:2]
    margin = jnp.minimum(donor - 1, most - taker)
    passed = jax.random.randint(jax.random.fold_in(rng, 1), (pairs,), 0, 1 << 20) % (margin + 1)
    lengths = lengths.at[1:1 + 2 * pairs:2].set(donor - passed).at[2:2 + 2 * pairs:2].set(taker + passed)
    return lengths[jax.random.permutation(jax.random.fold_in(rng, 2), number_of)]


def normal_values(key, extent, deviation, bound, split=(), kind=jnp.bfloat16):
    level = steps_of(key, extent, split, -0.22, 0.18) if split else 1.0
    values = jax.random.normal(key, extent, jnp.float32) * deviation * level
    return jnp.minimum(jnp.maximum(values, -bound), bound).astype(kind)


def setup_inputs(seed: int = 0) -> dict:
    seeds = jax.random.split(jax.random.key(seed), 7)
    activations = normal_values(seeds[0], (ALL_TOK, F), 1.0, 6.0, ((0, 16), (1, 8)))
    gradients = normal_values(seeds[1], (ALL_TOK, D), 0.00025, 0.0014953613, ((0, 8), (1, 16)))
    basis_in = normal_values(seeds[2], (F, F), F ** -0.5, 0.03125, ((0, 8), (1, 16)))
    basis_out = normal_values(seeds[3], (D, D), D ** -0.5, 0.0625, ((0, 16), (1, 8)))
    eigen_damped = jnp.clip(jnp.exp(math.log(4.0) - 3.6888794 * jax.random.uniform(seeds[4], (D, F), jnp.float32) ** steps_of(seeds[4], (D, F), ((0, 8), (1, 16)), -0.2, 0.2)), 0.1, 4.0)
    pair_ids = jnp.searchsorted(jnp.cumsum(uneven_parts(seeds[5], PAIRS, TOKENS, MOST, 1)), jnp.arange(TOKENS), side="right").astype(jnp.int32)
    return dict(activations=activations, gradients=gradients, basis_in=basis_in, basis_out=basis_out, eigen_damped=eigen_damped, pair_ids=pair_ids)


def rotate(values, basis, pieces):
    width = basis.shape[1] // pieces
    wide = values.astype(jnp.float32)
    parts = []
    for number in range(pieces):
        column_block = basis[:, number * width:(number + 1) * width].astype(jnp.float32)
        parts.append(jnp.dot(wide, column_block, precision=lax.Precision.HIGHEST))
    return jnp.concatenate(parts, axis=1).astype(jnp.bfloat16)


def reference(activations, gradients, basis_in, basis_out, eigen_damped, pair_ids):
    rotated_in = rotate(activations, basis_in, 8)
    rotated_out = rotate(gradients, basis_out, 1)
    pair_in = rotated_in[:TOKENS]
    pair_out = rotated_out[:TOKENS]
    query_in = rotated_in[TOKENS:].astype(jnp.float32)
    query_out = rotated_out[TOKENS:].astype(jnp.float32)
    labels = jnp.arange(PAIRS, dtype=jnp.int32)
    offsets = jnp.sum((pair_ids[None, :] < labels[:, None]).astype(jnp.int32), axis=1)

    def one_pair(pair_index):
        window_start = offsets[pair_index]
        window_out = lax.dynamic_slice_in_dim(pair_out, window_start, MOST, 0)
        window_in = lax.dynamic_slice_in_dim(pair_in, window_start, MOST, 0)
        window_ids = lax.dynamic_slice_in_dim(pair_ids, window_start, MOST, 0)
        window_out = jnp.where((window_ids == pair_index)[:, None], window_out, jnp.zeros_like(window_out))
        pair_block = jnp.dot(window_out.astype(jnp.float32).T, window_in.astype(jnp.float32), precision=lax.Precision.HIGHEST)
        scaled = (pair_block / eigen_damped).astype(jnp.bfloat16)
        mapped = jnp.dot(scaled.astype(jnp.float32), query_in.T, precision=lax.Precision.HIGHEST)
        per_token = jnp.sum(mapped * query_out.T, axis=0)
        return jnp.sum(per_token.reshape(QUERIES, QLEN), axis=1)

    return lax.map(one_pair, labels)
```

```python
import functools

import jax
import jax.numpy as jnp
from jax import lax
from jax.experimental import pallas as pl
from jax.experimental.pallas import tpu as pltpu
from jax.sharding import PartitionSpec as P

PAIRS = 4
QLEN = 4
MOST = 384
MESH = pl.DeviceIdType.MESH
BF16 = jnp.bfloat16
F32 = jnp.float32


def aligned(start, multiple, size):
    return pl.ds(pl.multiple_of(start, multiple), size)


class Place:
    def __init__(self):
        row, col = lax.axis_index("row"), lax.axis_index("col")
        self.xlo, self.y = row // 4, lax.rem(row, 4)
        self.z, self.xhi, self.core = col // 4, lax.rem(col // 2, 2), lax.rem(col, 2)

    def at(self, xlo=None, y=None, z=None, xhi=None, core=None):
        xlo = self.xlo if xlo is None else xlo
        y = self.y if y is None else y
        z = self.z if z is None else z
        xhi = self.xhi if xhi is None else xhi
        core = self.core if core is None else core
        return (xlo * 4 + y, z * 4 + xhi * 2 + core)


def remote(src, dst, sends, recvs, number, device):
    return pltpu.make_async_remote_copy(
        src_ref=src,
        dst_ref=dst,
        send_sem=sends.at[number],
        recv_sem=recvs.at[number],
        device_id=device,
        device_id_type=MESH,
    )


class Gather:
    def __init__(self, place, buf, slot, sends, recvs, first=None):
        zp, zm, z2 = (lax.rem(place.z + k, 4) for k in (1, 3, 2))
        xhi, other = place.xhi, 1 - place.xhi
        core, twin = place.core, 1 - place.core
        to_core, to_xhi = place.at(core=twin), place.at(xhi=other)
        to_zp, to_zm = place.at(z=zp), place.at(z=zm)
        z = place.z
        plan = [
            (z, xhi, to_core), (z, xhi, to_xhi), (z, xhi, to_zp), (z, xhi, to_zm),
            (z, other, to_core), (z, other, to_zp), (z, other, to_zm),
            (zm, xhi, to_core), (zm, xhi, to_zp), (zp, xhi, to_core),
            (zm, other, to_core), (zp, other, to_core), (zp, other, to_zm),
            (z2, xhi, to_core), (z2, other, to_core),
        ]
        self.copies = []
        for number, (from_z, from_x, device) in enumerate(plan):
            block = buf.at[slot(from_z, from_x, core)]
            src = first if number < 4 and first is not None else block
            self.copies.append(remote(src, block, sends, recvs, number, device))

    def start(self, *numbers):
        for number in numbers:
            self.copies[number].start()

    def wait(self, *numbers):
        for number in numbers:
            self.copies[number].wait_recv()

    def finish(self):
        for copy in self.copies:
            copy.wait_send()


def rotate_kernel(
    act, grad, basis_in, basis_out, rot_in_hbm, rot_out_hbm,
    a_buf, b_buf, part, send, land, land_x, rot_in,
    g_buf, bo_buf, part_out, land_core, land_z, land_h, rot_out,
    a_send, a_recv, d_send, d_recv, e_send, e_recv, f_send, f_recv, u_send, u_recv, local,
):
    me = Place()
    xlo, y, z, xhi, core = me.xlo, me.y, me.z, me.xhi, me.core
    yp, ym, y2 = (lax.rem(y + k, 4) for k in (1, 3, 2))
    zp, zm, z2 = (lax.rem(z + k, 4) for k in (1, 3, 2))
    to_yp, to_ym = me.at(y=yp), me.at(y=ym)
    to_zp, to_zm = me.at(z=zp), me.at(z=zm)
    to_xlo, to_xhi, to_core = me.at(xlo=1 - xlo), me.at(xhi=1 - xhi), me.at(core=1 - core)
    half = 896

    loads = [
        pltpu.make_async_copy(act, a_buf.at[aligned(80 * (4 * z + 2 * xhi + core), 80, 80)], local.at[0]),
        pltpu.make_async_copy(grad, g_buf.at[aligned(160 * (4 * xlo + y), 160, 160)], local.at[1]),
        pltpu.make_async_copy(basis_in, b_buf, local.at[2]),
        pltpu.make_async_copy(basis_out, bo_buf, local.at[3]),
    ]
    for load in loads:
        load.start()

    barrier = pltpu.get_barrier_semaphore()
    friends = (to_yp, to_ym, to_zp, to_zm, to_xlo, to_xhi, to_core)
    for friend in friends:
        pl.semaphore_signal(barrier, inc=1, device_id=friend, device_id_type=MESH)
    pl.semaphore_wait(barrier, len(friends))

    gather_a = Gather(
        me, a_buf, lambda gz, gx, gc: aligned(80 * (4 * gz + 2 * gx + gc), 80, 80), a_send, a_recv, act
    )
    gather_a.start(1, 2, 3, 0)

    def g_slot(gy, gx):
        return aligned(160 * (4 * gx + gy), 160, 160)

    def d_copy(number, rows, device, src=None):
        block = g_buf.at[rows]
        return remote(block if src is None else src, block, d_send, d_recv, number, device)

    d = [
        d_copy(0, g_slot(y, xlo), to_yp, grad),
        d_copy(1, g_slot(y, xlo), to_ym, grad),
        d_copy(2, g_slot(y, xlo), to_xlo, grad),
        d_copy(3, aligned(160 * (4 * xlo + ym), 80, 80), to_yp),
        d_copy(4, g_slot(ym, xlo), to_xlo),
        d_copy(5, aligned(160 * (4 * xlo + yp) + 80, 80, 80), to_ym),
        d_copy(6, g_slot(yp, xlo), to_xlo),
        d_copy(7, g_slot(y2, xlo), to_xlo),
    ]
    d[0].start()
    d[1].start()

    def gradients_on():
        d[0].wait_recv()
        d[3].start()
        d[1].wait_recv()
        d[5].start()

    def gradients_across():
        d[2].start()
        d[4].start()
        d[6].start()
        d[3].wait_recv()
        d[5].wait_recv()
        d[7].start()

    own = 640 * core

    def e_rows(ez):
        return aligned(own + 160 * ez, 160, 160)

    left, right = pl.ds(0, 512), pl.ds(512, 512)
    e0 = remote(
        part_out.at[aligned(640 * (1 - core), 640, 640)], land_core, e_send, e_recv, 0, to_core
    )
    e = [
        remote(part_out.at[e_rows(z2), left], land_z.at[0], e_send, e_recv, 1, to_zp),
        remote(part_out.at[e_rows(z2), right], land_z.at[1], e_send, e_recv, 2, to_zm),
        remote(part_out.at[e_rows(zm), left], land_z.at[2], e_send, e_recv, 3, to_zm),
        remote(part_out.at[e_rows(zp), right], land_z.at[3], e_send, e_recv, 4, to_zp),
        remote(part_out.at[e_rows(zp), left], land_z.at[4], e_send, e_recv, 5, to_zp),
        remote(part_out.at[e_rows(zm), right], land_z.at[5], e_send, e_recv, 6, to_zm),
    ]
    e_x = remote(
        part_out.at[aligned(own + 160 * z + 80 * (1 - xhi), 80, 80)], land_h, e_send, e_recv, 7, to_xhi
    )
    gather_f = Gather(
        me, rot_out, lambda gz, gx, gc: aligned(640 * gc + 160 * gz + 80 * gx, 80, 80), f_send, f_recv
    )

    def out_matmul():
        loads[1].wait()
        loads[3].wait()
        d[2].wait_recv()
        d[4].wait_recv()
        d[6].wait_recv()
        d[7].wait_recv()

        @pl.loop(0, 4)
        def _(n):
            rows = aligned(320 * n, 320, 320)
            part_out[rows, :] = jnp.dot(g_buf[rows, :], bo_buf[...], preferred_element_type=F32)

        e0.start()

    def out_core():
        e0.wait_recv()

        @pl.loop(0, 4)
        def _(n):
            rows = aligned(own + 160 * n, 160, 160)
            part_out[rows, :] += land_core[aligned(160 * n, 160, 160), :]

        for copy in e[:4]:
            copy.start()

    def out_z():
        e[0].wait_recv()
        part_out[e_rows(zp), left] += land_z[0]
        e[4].start()
        e[1].wait_recv()
        part_out[e_rows(zm), right] += land_z[1]
        e[5].start()

    def out_sum():
        for copy in e[2:]:
            copy.wait_recv()
        part_out[e_rows(z), left] += land_z[4] + land_z[2]
        part_out[e_rows(z), right] += land_z[5] + land_z[3]
        e_x.start()

    def out_final():
        e_x.wait_recv()
        rows = aligned(own + 160 * z + 80 * xhi, 80, 80)
        rot_out[rows, :] = (part_out[rows, :] + land_h[...]).astype(BF16)
        gather_f.start(1, 2, 3, 0)

    unit_z = (z, zm, zp, z2)
    everything = pl.ds(0, 1792)
    h0, h1 = pl.ds(0, half), pl.ds(half, half)
    mine, others = aligned(half * xlo, half, half), aligned(half * (1 - xlo), half, half)
    units = []
    for u in range(4):
        uz = unit_z[u]

        def rows_in_send(oy, uz=uz):
            return aligned(320 * uz + 80 * oy, 80, 80)

        def from_send(number, oy, cols, device, u=u):
            return remote(
                send.at[rows_in_send(oy), cols], land.at[u, number], u_send.at[u], u_recv.at[u], number, device
            )

        def spread(number, oy, cols, device, u=u):
            block = rot_in.at[rows_in_send(oy), cols]
            return remote(block, block, u_send.at[u], u_recv.at[u], number, device)

        units.append(
            [
                from_send(0, y2, h0, to_yp),
                from_send(1, y2, h1, to_ym),
                from_send(2, ym, h0, to_ym),
                from_send(3, yp, h1, to_yp),
                from_send(4, yp, h0, to_yp),
                from_send(5, ym, h1, to_ym),
                remote(
                    send.at[rows_in_send(y), others], land_x.at[u], u_send.at[u], u_recv.at[u], 6, to_xlo
                ),
                spread(7, y, mine, to_xlo),
                spread(8, y, mine, to_yp),
                spread(9, y, mine, to_ym),
                spread(10, y, others, to_yp),
                spread(11, y, others, to_ym),
                spread(12, ym, mine, to_yp),
                spread(13, yp, others, to_ym),
            ]
        )

    def matmul(u):
        rows = aligned(320 * unit_z[u], 320, 320)

        @pl.loop(0, 7)
        def _(n):
            cols = aligned(256 * n, 256, 256)
            block = jnp.dot(a_buf[rows, :], b_buf[:, cols], preferred_element_type=F32)
            part[u % 2, :, cols] = block
            send[rows, cols] = block.astype(BF16)

        for copy in units[u][:4]:
            copy.start()

    def part_rows(oy):
        return aligned(80 * oy, 80, 80)

    def send_rows(u, oy):
        return aligned(320 * unit_z[u] + 80 * oy, 80, 80)

    def second(u):
        c = units[u]
        c[0].wait_recv()
        send[send_rows(u, yp), h0] = (part[u % 2, part_rows(yp), h0] + land[u, 0].astype(F32)).astype(BF16)
        c[4].start()
        c[1].wait_recv()
        send[send_rows(u, ym), h1] = (part[u % 2, part_rows(ym), h1] + land[u, 1].astype(F32)).astype(BF16)
        c[5].start()

    def third(u):
        c = units[u]
        for number in (2, 3, 4, 5):
            c[number].wait_recv()
        rows = part_rows(y)
        part[u % 2, rows, h0] += land[u, 4].astype(F32) + land[u, 2].astype(F32)
        part[u % 2, rows, h1] += land[u, 5].astype(F32) + land[u, 3].astype(F32)
        send[send_rows(u, y), others] = part[u % 2, rows, others].astype(BF16)
        c[6].start()

    def fourth(u):
        c = units[u]
        c[6].wait_recv()
        rot_in[send_rows(u, y), mine] = (part[u % 2, part_rows(y), mine] + land_x[u].astype(F32)).astype(BF16)
        for number in (7, 8, 9):
            c[number].start()

    def fifth(u):
        c = units[u]
        c[7].wait_recv()
        c[10].start()
        c[11].start()

    def sixth(u):
        c = units[u]
        c[8].wait_recv()
        c[12].start()
        c[11].wait_recv()
        c[13].start()

    def last(u):
        c = units[u]
        for number in (9, 10, 12, 13):
            c[number].wait_recv()

    gradients_on()
    loads[0].wait()
    gather_a.wait(1)
    gather_a.start(4, 5, 6)
    gather_a.wait(2)
    gather_a.start(8, 7)
    gather_a.wait(3)
    gather_a.start(9)
    gradients_across()
    loads[2].wait()
    gather_a.wait(0, 4)
    matmul(0)
    second(0)
    gather_a.wait(5)
    gather_a.start(10)
    gather_a.wait(6)
    gather_a.start(12, 11)
    third(0)
    gather_a.wait(7, 10)
    matmul(1)
    fourth(0)
    gather_a.wait(9, 11)
    fifth(0)
    second(1)
    sixth(0)
    third(1)
    matmul(2)
    gather_a.wait(8)
    gather_a.start(13)
    gather_a.wait(12)
    gather_a.start(14)
    fourth(1)
    out_matmul()
    second(2)
    out_core()
    fifth(1)
    gather_a.wait(13, 14)
    third(2)
    sixth(1)
    matmul(3)
    fourth(2)
    out_z()
    fifth(2)
    second(3)
    sixth(2)
    out_sum()
    third(3)
    out_final()
    fourth(3)
    gather_f.wait(1)
    gather_f.start(4, 5, 6)
    gather_f.wait(2)
    gather_f.start(8, 7)
    gather_f.wait(3)
    gather_f.start(9)
    fifth(3)
    gather_f.wait(5)
    gather_f.start(10)
    gather_f.wait(6)
    gather_f.start(12, 11)
    sixth(3)
    gather_f.wait(8)
    gather_f.start(13)
    gather_f.wait(12)
    gather_f.start(14)
    gather_f.wait(0, 4, 7, 9, 10, 11, 13, 14)
    out_store = pltpu.make_async_copy(rot_out, rot_out_hbm, local.at[4])
    out_store.start()
    for u in range(4):
        last(u)
    in_store = pltpu.make_async_copy(rot_in, rot_in_hbm, local.at[5])
    in_store.start()
    gather_a.finish()
    gather_f.finish()
    for copy in d + [e0, e_x] + e:
        copy.wait_send()
    for c in units:
        for copy in c:
            copy.wait_send()
    out_store.wait()
    in_store.wait()


def rotate(activations, gradients, basis_in, basis_out):
    anywhere = pl.BlockSpec(memory_space=pl.ANY)
    dma = pltpu.SemaphoreType.DMA
    return pl.pallas_call(
        rotate_kernel,
        out_shape=(jax.ShapeDtypeStruct((1280, 1792), BF16), jax.ShapeDtypeStruct((1280, 1024), BF16)),
        in_specs=[anywhere] * 4,
        out_specs=(anywhere, anywhere),
        scratch_shapes=[
            pltpu.VMEM((1280, 3584), BF16),
            pltpu.VMEM((3584, 1792), BF16),
            pltpu.VMEM((2, 320, 1792), F32),
            pltpu.VMEM((1280, 1792), BF16),
            pltpu.VMEM((4, 6, 80, 896), BF16),
            pltpu.VMEM((4, 80, 896), BF16),
            pltpu.VMEM((1280, 1792), BF16),
            pltpu.VMEM((1280, 512), BF16),
            pltpu.VMEM((512, 1024), BF16),
            pltpu.VMEM((1280, 1024), F32),
            pltpu.VMEM((640, 1024), F32),
            pltpu.VMEM((6, 160, 512), F32),
            pltpu.VMEM((80, 1024), F32),
            pltpu.VMEM((1280, 1024), BF16),
            dma((15,)), dma((15,)),
            dma((8,)), dma((8,)),
            dma((8,)), dma((8,)),
            dma((15,)), dma((15,)),
            dma((4, 14)), dma((4, 14)),
            dma((6,)),
        ],
        compiler_params=pltpu.CompilerParams(
            collective_id=0, has_side_effects=True, vmem_limit_bytes=60 * 2**20
        ),
        cost_estimate=pl.CostEstimate(flops=18 * 10**9, bytes_accessed=22 * 10**6, transcendentals=0),
    )(activations, gradients, basis_in, basis_out)


def on_device(activations, gradients, basis_in, basis_out, eigen_damped, pair_ids):
    pair_rows = pair_ids.shape[0]
    rotated_in, rotated_out = rotate(activations, gradients, basis_in, basis_out)
    pair_in = rotated_in[:pair_rows]
    pair_out = rotated_out[:pair_rows]
    query_in = rotated_in[pair_rows:]
    query_out = rotated_out[pair_rows:].astype(jnp.float32)
    labels = jnp.arange(PAIRS, dtype=jnp.int32)
    offsets = jnp.sum((pair_ids[None, :] < labels[:, None]).astype(jnp.int32), axis=1)
    scaled_list = []
    for pair_index in range(PAIRS):
        window_start = offsets[pair_index]
        window_out = lax.dynamic_slice_in_dim(pair_out, window_start, MOST, 0)
        window_in = lax.dynamic_slice_in_dim(pair_in, window_start, MOST, 0)
        window_ids = lax.dynamic_slice_in_dim(pair_ids, window_start, MOST, 0)
        window_out = jnp.where(
            (window_ids == pair_index)[:, None], window_out, jnp.zeros_like(window_out)
        )
        pair_block = lax.dot_general(
            window_out, window_in, (((0,), (0,)), ((), ())), preferred_element_type=jnp.float32
        )
        scaled_list.append((pair_block / eigen_damped).astype(jnp.bfloat16))
    scaled = jnp.stack(scaled_list)
    mapped = jnp.einsum("pif,sf->pis", scaled, query_in, preferred_element_type=jnp.float32)
    per_token = jnp.sum(mapped * query_out.T[None, :, :], axis=1)
    partial_scores = jnp.sum(per_token.reshape(PAIRS, -1, QLEN), axis=2)
    return lax.psum(partial_scores, ("row", "col"))


def solution(mesh):
    return jax.shard_map(
        on_device,
        mesh=mesh,
        in_specs=(
            P("col", "row"),
            P("row", "col"),
            P("row", "col"),
            P("col", "row"),
            P("row", "col"),
            P(),
        ),
        out_specs=P(),
        check_vma=False,
    )
```

```python
import functools

import jax
import jax.numpy as jnp
from jax import lax
from jax.experimental import pallas as pl
from jax.experimental.pallas import tpu as pltpu
from jax.sharding import PartitionSpec as P

PAIRS = 4
QLEN = 4
WINDOWS = ((0, 384, 0), (0, 768, 384), (256, 1024, 1152), (640, 1024, 1920))
QUERY_AT = 2304
HALF = 896
SLOTS = 5
MESH = pl.DeviceIdType.MESH
BF16 = jnp.bfloat16
F32 = jnp.float32


def aligned(start, multiple, size):
    return pl.ds(pl.multiple_of(start, multiple), size)


class Place:
    def __init__(self):
        row, col = lax.axis_index("row"), lax.axis_index("col")
        self.xlo, self.y = row // 4, lax.rem(row, 4)
        self.z, self.xhi, self.core = col // 4, lax.rem(col // 2, 2), lax.rem(col, 2)

    def at(self, xlo=None, y=None, z=None, xhi=None, core=None):
        xlo = self.xlo if xlo is None else xlo
        y = self.y if y is None else y
        z = self.z if z is None else z
        xhi = self.xhi if xhi is None else xhi
        core = self.core if core is None else core
        return (xlo * 4 + y, z * 4 + xhi * 2 + core)


def remote(src, dst, sends, recvs, number, device):
    return pltpu.make_async_remote_copy(
        src_ref=src,
        dst_ref=dst,
        send_sem=sends.at[number],
        recv_sem=recvs.at[number],
        device_id=device,
        device_id_type=MESH,
    )


class Gather:
    def __init__(self, place, buf, slot, sends, recvs, first=None):
        zp, zm, z2 = (lax.rem(place.z + k, 4) for k in (1, 3, 2))
        xhi, other = place.xhi, 1 - place.xhi
        core, twin = place.core, 1 - place.core
        to_core, to_xhi = place.at(core=twin), place.at(xhi=other)
        to_zp, to_zm = place.at(z=zp), place.at(z=zm)
        z = place.z
        plan = [
            (z, xhi, to_core), (z, xhi, to_xhi), (z, xhi, to_zp), (z, xhi, to_zm),
            (z, other, to_core), (z, other, to_zp), (z, other, to_zm),
            (zm, xhi, to_core), (zm, xhi, to_zp), (zp, xhi, to_core),
            (zm, other, to_core), (zp, other, to_core), (zp, other, to_zm),
            (z2, xhi, to_core), (z2, other, to_core),
        ]
        self.copies = []
        for number, (from_z, from_x, device) in enumerate(plan):
            block = buf.at[slot(from_z, from_x, core)]
            src = first if number < 4 and first is not None else block
            self.copies.append(remote(src, block, sends, recvs, number, device))

    def start(self, *numbers):
        for number in numbers:
            self.copies[number].start()

    def wait(self, *numbers):
        for number in numbers:
            self.copies[number].wait_recv()

    def finish(self):
        for copy in self.copies:
            copy.wait_send()


ORDER = (
    ("rcp", "mm0", "Da", "Db", "sb0", "sa0", "A1", "A2", "A3", "Dc", "th0", "mm1", "sb1", "sa1", "A5", "A6"),
    ("th1", "Dx", "mm2", "outmm", "fo0", "fo1", "sb2", "mm3", "A8", "sa2", "mm5", "A12", "fa0", "fb0"),
    ("fa1", "fb1", "mm6", "sb3", "sa3", "mm4", "th2", "sa5", "sb5", "outa", "outb", "la0", "la1", "sb6"),
    ("fo2", "mm7", "th3", "sb4", "sa6", "sa4", "outsum", "th5", "fo3", "fa2", "sb7", "fb2", "sa7", "th6"),
    ("outfin", "th4", "fo5", "fb3", "fa3", "F2", "F3", "la2", "fo6", "th7", "fa5", "F1", "fb5", "F8", "la3"),
    ("fo4", "fa6", "fb6", "F5", "F6", "fo7", "la5", "fb4", "fa4", "F12", "la6", "Fdone", "prep", "fa7"),
    ("fb7", "la4", "fin0", "la7", "fin1"),
)


def kernel(
    act, grad, basis_in, basis_out, eigen, ids, scores,
    a_buf, b_buf, part, send, land, rot_in,
    g_buf, g_twin, bo_buf, bo_twin, part_out, land_z, land_h, rot_out,
    eig, acc, red_row, red_col,
    a_send, a_recv, d_send, d_recv, e_send, e_recv, f_send, f_recv, u_send, u_recv,
    r_send, r_recv, c_send, c_recv, local,
):
    me = Place()
    row, col = lax.axis_index("row"), lax.axis_index("col")
    xlo, y, z, xhi, core = me.xlo, me.y, me.z, me.xhi, me.core
    yp, ym, y2 = (lax.rem(y + k, 4) for k in (1, 3, 2))
    zp, zm, z2 = (lax.rem(z + k, 4) for k in (1, 3, 2))
    to_yp, to_ym = me.at(y=yp), me.at(y=ym)
    to_zp, to_zm = me.at(z=zp), me.at(z=zm)
    to_xlo, to_xhi, to_core = me.at(xlo=1 - xlo), me.at(xhi=1 - xhi), me.at(core=1 - core)
    row_mates = [(lax.rem(row + k, 8), col) for k in range(1, 8)]
    col_mates = [(row, lax.rem(col + k, 16)) for k in range(1, 16)]

    loads = {
        "act": pltpu.make_async_copy(act, a_buf.at[aligned(80 * (4 * z + 2 * xhi + core), 80, 80)], local.at[0]),
        "grad": pltpu.make_async_copy(grad, g_buf.at[aligned(160 * (4 * xlo + y), 160, 160)], local.at[1]),
        "basis_in": pltpu.make_async_copy(basis_in, b_buf, local.at[2]),
        "basis_out": pltpu.make_async_copy(basis_out, bo_buf, local.at[3]),
        "eigen": pltpu.make_async_copy(eigen, eig, local.at[4]),
    }
    for load in loads.values():
        load.start()

    barrier = pltpu.get_barrier_semaphore()
    for mate in row_mates + col_mates:
        pl.semaphore_signal(barrier, inc=1, device_id=mate, device_id_type=MESH)
    pl.semaphore_wait(barrier, len(row_mates) + len(col_mates))

    ops = {}

    gather_a = Gather(
        me, a_buf, lambda gz, gx, gc: aligned(80 * (4 * gz + 2 * gx + gc), 80, 80), a_send, a_recv, act
    )
    gather_f = Gather(
        me, rot_out, lambda gz, gx, gc: aligned(640 * gc + 160 * gz + 80 * gx, 80, 80), f_send, f_recv
    )
    onward = {1: (5, 6, 4), 2: (8, 7), 3: (9,), 5: (10,), 6: (12, 11), 8: (13,), 12: (14,)}

    def forward(gather, number):
        gather.wait(number)
        gather.start(*onward[number])

    for number in onward:
        ops["A%d" % number] = functools.partial(forward, gather_a, number)
        ops["F%d" % number] = functools.partial(forward, gather_f, number)

    def g_slot(gy, gx):
        return aligned(160 * (4 * gx + gy), 160, 160)

    def d_copy(number, rows, device, src=None):
        block = g_buf.at[rows]
        return remote(block if src is None else src, block, d_send, d_recv, number, device)

    d = [
        d_copy(0, g_slot(y, xlo), to_yp, grad),
        d_copy(1, g_slot(y, xlo), to_ym, grad),
        d_copy(2, g_slot(y, xlo), to_xlo, grad),
        d_copy(3, aligned(160 * (4 * xlo + ym), 80, 80), to_yp),
        d_copy(4, g_slot(ym, xlo), to_xlo),
        d_copy(5, aligned(160 * (4 * xlo + yp) + 80, 80, 80), to_ym),
        d_copy(6, g_slot(yp, xlo), to_xlo),
        d_copy(7, g_slot(y2, xlo), to_xlo),
        remote(g_buf.at[aligned(640 * (1 - core), 640, 640)], g_twin, d_send, d_recv, 8, to_core),
        remote(basis_out, bo_twin, d_send, d_recv, 9, to_core),
    ]

    def gradients_a():
        d[0].wait_recv()
        d[3].start()

    def gradients_b():
        d[1].wait_recv()
        d[5].start()

    def gradients_c():
        d[3].wait_recv()
        d[5].wait_recv()
        for number in (2, 4, 6, 7):
            d[number].start()

    def gradients_x():
        for number in (2, 4, 6, 7):
            d[number].wait_recv()
        loads["grad"].wait()
        d[8].start()

    ops.update(Da=gradients_a, Db=gradients_b, Dc=gradients_c, Dx=gradients_x)

    def e_rows(ez):
        return aligned(160 * ez, 160, 160)

    left, right = pl.ds(0, 512), pl.ds(512, 512)
    e = [
        remote(part_out.at[e_rows(z2), left], land_z.at[0], e_send, e_recv, 0, to_zp),
        remote(part_out.at[e_rows(z2), right], land_z.at[1], e_send, e_recv, 1, to_zm),
        remote(part_out.at[e_rows(zm), left], land_z.at[2], e_send, e_recv, 2, to_zm),
        remote(part_out.at[e_rows(zp), right], land_z.at[3], e_send, e_recv, 3, to_zp),
        remote(part_out.at[e_rows(zp), left], land_z.at[4], e_send, e_recv, 4, to_zp),
        remote(part_out.at[e_rows(zm), right], land_z.at[5], e_send, e_recv, 5, to_zm),
        remote(part_out.at[aligned(160 * z + 80 * (1 - xhi), 80, 80)], land_h, e_send, e_recv, 6, to_xhi),
    ]

    def out_matmul():
        loads["basis_out"].wait()
        d[8].wait_recv()
        d[9].wait_recv()

        @pl.loop(0, 4)
        def _(n):
            rows = aligned(160 * n, 160, 160)
            part_out[rows, :] = jnp.dot(
                g_buf[aligned(640 * core + 160 * n, 160, 160), :], bo_buf[...], preferred_element_type=F32
            ) + jnp.dot(g_twin[rows, :], bo_twin[...], preferred_element_type=F32)

        for copy in e[:4]:
            copy.start()

    def out_a():
        e[0].wait_recv()
        part_out[e_rows(zp), left] += land_z[0]
        e[4].start()

    def out_b():
        e[1].wait_recv()
        part_out[e_rows(zm), right] += land_z[1]
        e[5].start()

    def out_sum():
        for copy in e[2:6]:
            copy.wait_recv()
        part_out[e_rows(z), left] += land_z[4] + land_z[2]
        part_out[e_rows(z), right] += land_z[5] + land_z[3]
        e[6].start()

    def out_final():
        e[6].wait_recv()
        rot_out[aligned(640 * core + 160 * z + 80 * xhi, 80, 80), :] = (
            part_out[aligned(160 * z + 80 * xhi, 80, 80), :] + land_h[...]
        ).astype(BF16)
        gather_f.start(1, 2, 3, 0)

    def out_done():
        gather_f.wait(0, 4, 7, 9, 10, 11, 13, 14)

    ops.update(outmm=out_matmul, outa=out_a, outb=out_b, outsum=out_sum, outfin=out_final, Fdone=out_done)

    class Unit:
        def __init__(self, u):
            self.u, self.slot = u, u % SLOTS
            if u < 2:
                self.start = 160 * (2 * z + (xhi, 1 - xhi)[u])
                self.need = ((0,), (4,))[u]
            else:
                self.start = 320 * (zm, zp, z2)[(u - 2) % 3]
                self.need = ((7, 10), (9, 11), (13, 14))[(u - 2) % 3] if u < 5 else ()
            big, small = pl.ds(0, 48), pl.ds(48, 32)
            self.h = (big, small)
            if u % 2 == 0:
                self.up, self.down, to_up, to_down = yp, ym, to_yp, to_ym
                onward_a, onward_b = (48, 32), (0, 48)
            else:
                self.up, self.down, to_up, to_down = ym, yp, to_ym, to_yp
                onward_a, onward_b = (0, 48), (48, 32)

            def term(number, owner, rows, where, device):
                return remote(
                    send.at[u, owner, rows], land.at[u, where, rows], u_send.at[u], u_recv.at[u], number, device
                )

            def spread(number, owner, device, offset=0, count=80):
                block = rot_in.at[self.place(owner, offset, count)]
                return remote(block, block, u_send.at[u], u_recv.at[u], number, device)

            self.copies = [
                term(0, y2, big, 0, to_up),
                term(1, y2, small, 0, to_down),
                term(2, self.down, big, 1, to_down),
                term(3, self.up, small, 1, to_up),
                term(4, self.up, big, 2, to_up),
                term(5, self.down, small, 2, to_down),
                remote(send.at[u, y], land.at[u, 3], u_send.at[u], u_recv.at[u], 6, to_xlo),
                spread(7, y, to_yp),
                spread(8, y, to_ym),
                spread(9, ym, to_yp, *onward_a),
                spread(10, yp, to_ym, *onward_b),
            ]

        def place(self, owner, offset=0, count=80):
            if self.u < 2:
                rows = aligned(self.start + 80 * (owner // 2) + offset, 16, count)
                return rows, aligned(HALF * lax.rem(owner, 2), 128, HALF)
            return aligned(self.start + 80 * owner + offset, 16, count), pl.ds(HALF * ((self.u - 2) // 3), HALF)

        def matmul(self):
            if self.u == 0:
                loads["act"].wait()
                loads["basis_in"].wait()
            gather_a.wait(*self.need)
            if self.u < 2:
                rows = aligned(self.start, 160, 160)

                @pl.loop(0, 2)
                def _(n):
                    block = jnp.dot(
                        a_buf[rows, :], b_buf[:, aligned(HALF * n, HALF, HALF)], preferred_element_type=F32
                    )
                    for half in range(2):
                        piece = block[80 * half:80 * half + 80]
                        part[self.slot, 2 * half + n] = piece
                        send[self.u, 2 * half + n] = piece.astype(BF16)
            else:
                block = jnp.dot(
                    a_buf[aligned(self.start, 320, 320), :],
                    b_buf[:, HALF * ((self.u - 2) // 3):HALF * ((self.u - 2) // 3) + HALF],
                    preferred_element_type=F32,
                )
                for owner in range(4):
                    piece = block[80 * owner:80 * owner + 80]
                    part[self.slot, owner] = piece
                    send[self.u, owner] = piece.astype(BF16)
            for copy in self.copies[:4]:
                copy.start()

        def second(self, number):
            owner, rows = ((self.up, self.h[0]), (self.down, self.h[1]))[number]
            self.copies[number].wait_recv()
            send[self.u, owner, rows] = (
                part[self.slot, owner, rows] + land[self.u, 0, rows].astype(F32)
            ).astype(BF16)
            self.copies[4 + number].start()

        def third(self):
            for number in (2, 3, 4, 5):
                self.copies[number].wait_recv()
            total = part[self.slot, y] + (land[self.u, 1].astype(F32) + land[self.u, 2].astype(F32))
            part[self.slot, y] = total
            send[self.u, y] = total.astype(BF16)
            self.copies[6].start()

        def fourth(self):
            self.copies[6].wait_recv()
            rot_in[self.place(y)] = (part[self.slot, y] + land[self.u, 3].astype(F32)).astype(BF16)
            self.copies[7].start()
            self.copies[8].start()

        def spread_on(self, number):
            self.copies[7 + number].wait_recv()
            self.copies[9 + number].start()

        def last(self):
            self.copies[9].wait_recv()
            self.copies[10].wait_recv()

    units = [Unit(u) for u in range(8)]
    for u, unit in enumerate(units):
        ops["mm%d" % u] = unit.matmul
        ops["sa%d" % u] = functools.partial(unit.second, 0)
        ops["sb%d" % u] = functools.partial(unit.second, 1)
        ops["th%d" % u] = unit.third
        ops["fo%d" % u] = unit.fourth
        ops["fa%d" % u] = functools.partial(unit.spread_on, 0)
        ops["fb%d" % u] = functools.partial(unit.spread_on, 1)
        ops["la%d" % u] = unit.last

    def reciprocal():
        loads["eigen"].wait()

        @pl.loop(0, 16)
        def _(n):
            rows = aligned(64 * n, 64, 64)
            eig[rows, :] = 1.0 / eig[rows, :]

    def prepare():
        gather_a.finish()

        @pl.loop(0, 4)
        def _(n):
            rows = aligned(256 * n, 256, 256)
            turned = rot_out[:, rows].astype(F32).T
            for p, (first, last, at) in enumerate(WINDOWS):
                kept = jnp.where(ids[0:1, first:last] == p, turned[:, first:last], 0.0)
                a_buf[rows, at:at + last - first] = kept.astype(BF16)
            a_buf[rows, QUERY_AT:QUERY_AT + 256] = turned[:, 1024:1280].astype(BF16)

        acc[...] = jnp.zeros_like(acc)

    def final(half):
        cols = slice(HALF * half, HALF * half + HALF)
        for p, (first, last, at) in enumerate(WINDOWS):

            @pl.loop(0, 4)
            def _(n):
                rows = aligned(256 * n, 256, 256)
                pair_block = jnp.dot(
                    a_buf[rows, at:at + last - first], rot_in[first:last, cols], preferred_element_type=F32
                )
                scaled = (pair_block * eig[rows, cols]).astype(BF16)
                mapped = lax.dot_general(
                    scaled, rot_in[1024:1280, cols], (((1,), (1,)), ((), ())), preferred_element_type=F32
                )
                query = a_buf[rows, QUERY_AT:QUERY_AT + 256].astype(F32)
                acc[p:p + 1, :] += jnp.sum(mapped * query, axis=0, keepdims=True)

    ops.update(rcp=reciprocal, prep=prepare, fin0=functools.partial(final, 0), fin1=functools.partial(final, 1))

    gather_a.start(1, 2, 3, 0)
    d[0].start()
    d[1].start()
    d[9].start()
    for names in ORDER:
        for name in names:
            ops[name]()

    token = lax.broadcasted_iota(jnp.int32, (256, 128), 0)
    query = lax.broadcasted_iota(jnp.int32, (256, 128), 1)
    pick = jnp.where(token // QLEN == query, 1.0, 0.0)
    red_row[row] = jnp.dot(acc[...], pick, precision=lax.Precision.HIGHEST, preferred_element_type=F32)

    def everyone(red, position, mates, sends, recvs):
        copies = []
        for k, mate in enumerate(mates):
            copies.append(remote(red.at[position], red.at[position], sends, recvs, k, mate))
        for copy in copies:
            copy.start()
        for copy in copies:
            copy.wait_recv()
        return copies

    row_copies = everyone(red_row, row, row_mates, r_send, r_recv)
    red_col[col] = jnp.sum(red_row[...], axis=0)
    col_copies = everyone(red_col, col, col_mates, c_send, c_recv)
    scores[...] = jnp.sum(red_col[...], axis=0)[:PAIRS, :64]

    gather_f.finish()
    for copy in d + e + row_copies + col_copies:
        copy.wait_send()
    for unit in units:
        for copy in unit.copies:
            copy.wait_send()


def on_device(activations, gradients, basis_in, basis_out, eigen_damped, pair_ids):
    anywhere = pl.BlockSpec(memory_space=pl.ANY)
    vmem = pl.BlockSpec(memory_space=pltpu.VMEM)
    dma = pltpu.SemaphoreType.DMA
    return pl.pallas_call(
        kernel,
        out_shape=jax.ShapeDtypeStruct((PAIRS, 64), F32),
        in_specs=[anywhere] * 5 + [vmem],
        out_specs=vmem,
        scratch_shapes=[
            pltpu.VMEM((1280, 3584), BF16),
            pltpu.VMEM((3584, 1792), BF16),
            pltpu.VMEM((SLOTS, 4, 80, HALF), F32),
            pltpu.VMEM((8, 4, 80, HALF), BF16),
            pltpu.VMEM((8, 4, 80, HALF), BF16),
            pltpu.VMEM((1280, 1792), BF16),
            pltpu.VMEM((1280, 512), BF16),
            pltpu.VMEM((640, 512), BF16),
            pltpu.VMEM((512, 1024), BF16),
            pltpu.VMEM((512, 1024), BF16),
            pltpu.VMEM((640, 1024), F32),
            pltpu.VMEM((6, 160, 512), F32),
            pltpu.VMEM((80, 1024), F32),
            pltpu.VMEM((1280, 1024), BF16),
            pltpu.VMEM((1024, 1792), F32),
            pltpu.VMEM((8, 256), F32),
            pltpu.VMEM((8, 8, 128), F32),
            pltpu.VMEM((16, 8, 128), F32),
            dma((15,)), dma((15,)),
            dma((10,)), dma((10,)),
            dma((7,)), dma((7,)),
            dma((15,)), dma((15,)),
            dma((8, 11)), dma((8, 11)),
            dma((7,)), dma((7,)),
            dma((15,)), dma((15,)),
            dma((5,)),
        ],
        compiler_params=pltpu.CompilerParams(
            collective_id=0, has_side_effects=True, vmem_limit_bytes=63 * 2**20
        ),
        cost_estimate=pl.CostEstimate(flops=28 * 10**9, bytes_accessed=22 * 10**6, transcendentals=0),
    )(activations, gradients, basis_in, basis_out, eigen_damped, pair_ids.reshape(1, 1024))


def solution(mesh):
    return jax.shard_map(
        on_device,
        mesh=mesh,
        in_specs=(
            P("col", "row"),
            P("row", "col"),
            P("row", "col"),
            P("col", "row"),
            P("row", "col"),
            P(),
        ),
        out_specs=P(),
        check_vma=False,
    )
```

```python
import functools

import jax
import jax.numpy as jnp
from jax import lax
from jax.experimental import pallas as pl
from jax.experimental.pallas import tpu as pltpu
from jax.sharding import PartitionSpec as P

PAIRS = 4
QLEN = 4
WINDOWS = ((0, 384, 0), (0, 768, 384), (256, 1024, 1152), (640, 1024, 1920))
QUERY_AT = 2304
HALF = 896
SLOTS = 5
MESH = pl.DeviceIdType.MESH
BF16 = jnp.bfloat16
F32 = jnp.float32


def aligned(start, multiple, size):
    return pl.ds(pl.multiple_of(start, multiple), size)


class Place:
    def __init__(self):
        row, col = lax.axis_index("row"), lax.axis_index("col")
        self.xlo, self.y = row // 4, lax.rem(row, 4)
        self.z, self.xhi, self.core = col // 4, lax.rem(col // 2, 2), lax.rem(col, 2)

    def at(self, xlo=None, y=None, z=None, xhi=None, core=None):
        xlo = self.xlo if xlo is None else xlo
        y = self.y if y is None else y
        z = self.z if z is None else z
        xhi = self.xhi if xhi is None else xhi
        core = self.core if core is None else core
        return (xlo * 4 + y, z * 4 + xhi * 2 + core)


def remote(src, dst, sends, recvs, number, device):
    return pltpu.make_async_remote_copy(
        src_ref=src,
        dst_ref=dst,
        send_sem=sends.at[number],
        recv_sem=recvs.at[number],
        device_id=device,
        device_id_type=MESH,
    )


class Gather:
    def __init__(self, place, buf, slot, sends, recvs, first=None):
        zp, zm, z2 = (lax.rem(place.z + k, 4) for k in (1, 3, 2))
        xhi, other = place.xhi, 1 - place.xhi
        core, twin = place.core, 1 - place.core
        to_core, to_xhi = place.at(core=twin), place.at(xhi=other)
        to_zp, to_zm = place.at(z=zp), place.at(z=zm)
        z = place.z
        plan = [
            (z, xhi, to_core), (z, xhi, to_xhi), (z, xhi, to_zp), (z, xhi, to_zm),
            (z, other, to_core), (z, other, to_zp), (z, other, to_zm),
            (zm, xhi, to_core), (zm, xhi, to_zp), (zp, xhi, to_core),
            (zm, other, to_core), (zp, other, to_core), (zp, other, to_zm),
            (z2, xhi, to_core), (z2, other, to_core),
        ]
        self.copies = []
        for number, (from_z, from_x, device) in enumerate(plan):
            block = buf.at[slot(from_z, from_x, core)]
            src = first if number < 4 and first is not None else block
            self.copies.append(remote(src, block, sends, recvs, number, device))

    def start(self, *numbers):
        for number in numbers:
            self.copies[number].start()

    def wait(self, *numbers):
        for number in numbers:
            self.copies[number].wait_recv()

    def finish(self):
        for copy in self.copies:
            copy.wait_send()


ORDER = (
    ("Ax", "Db", "Da", "mm0", "Dc2", "Dc4", "sb0", "A1", "Dc7", "sa0", "mm1", "Dc6", "rcp", "sb1", "A2", "th0"),
    ("A3", "A6", "Dx", "sa1", "A5", "mm3", "mm2", "outmm", "sa3", "sb2", "A8", "th1", "sa2", "A12", "fo0", "sb3"),
    ("mm5", "fo1", "th2", "outb", "sa5", "th3", "sb5", "outa", "fo2", "mm7", "mm4", "th5", "outsum", "fo3"),
    ("sa4", "sb7", "sb4", "fb1", "mm6", "fa2", "sa7", "fo5", "outfin", "go5", "sb6", "sa6", "fa0", "fa1", "th4"),
    ("th7", "fb2", "fb3", "F1", "fa5", "fb5", "fa3", "fb0", "F2", "fo4", "th6", "F3", "F6", "F8", "fo7", "la3"),
    ("F5", "la1", "F12", "fo6", "fb4", "gb5", "fa4", "go6", "la2", "la5", "go7", "fa7", "la0", "Fdone", "prep"),
    ("fa6", "ga5", "la4", "fb7", "fb6", "fin0", "ga6", "gb6", "la6", "la7", "gb7", "ga7", "fin1", "ka5", "ka6"),
    ("ka7", "fin2"),
)


def kernel(
    act, grad, basis_in, basis_out, eigen, ids, scores,
    a_buf, b_buf, part, send, land, rot_in,
    g_buf, g_twin, bo_buf, bo_twin, part_out, land_z, land_h, rot_out,
    eig, acc, red_row, red_col,
    a_send, a_recv, d_send, d_recv, e_send, e_recv, f_send, f_recv, u_send, u_recv,
    r_send, r_recv, c_send, c_recv, local,
):
    me = Place()
    row, col = lax.axis_index("row"), lax.axis_index("col")
    xlo, y, z, xhi, core = me.xlo, me.y, me.z, me.xhi, me.core
    yp, ym, y2 = (lax.rem(y + k, 4) for k in (1, 3, 2))
    zp, zm, z2 = (lax.rem(z + k, 4) for k in (1, 3, 2))
    to_yp, to_ym = me.at(y=yp), me.at(y=ym)
    to_zp, to_zm = me.at(z=zp), me.at(z=zm)
    to_xlo, to_xhi, to_core = me.at(xlo=1 - xlo), me.at(xhi=1 - xhi), me.at(core=1 - core)
    row_mates = [(lax.rem(row + k, 8), col) for k in range(1, 8)]
    col_mates = [(row, lax.rem(col + k, 16)) for k in range(1, 16)]

    loads = {
        "act": pltpu.make_async_copy(act, a_buf.at[aligned(80 * (4 * z + 2 * xhi + core), 80, 80)], local.at[0]),
        "grad": pltpu.make_async_copy(grad, g_buf.at[aligned(160 * (4 * xlo + y), 160, 160)], local.at[1]),
        "basis_in": pltpu.make_async_copy(basis_in, b_buf, local.at[2]),
        "basis_out": pltpu.make_async_copy(basis_out, bo_buf, local.at[3]),
        "eigen": pltpu.make_async_copy(eigen, eig, local.at[4]),
    }
    for load in loads.values():
        load.start()

    barrier = pltpu.get_barrier_semaphore()
    for mate in row_mates + col_mates:
        pl.semaphore_signal(barrier, inc=1, device_id=mate, device_id_type=MESH)
    pl.semaphore_wait(barrier, len(row_mates) + len(col_mates))

    ops = {}

    gather_a = Gather(
        me, a_buf, lambda gz, gx, gc: aligned(80 * (4 * gz + 2 * gx + gc), 80, 80), a_send, a_recv, act
    )
    gather_f = Gather(
        me, rot_out, lambda gz, gx, gc: aligned(640 * gc + 160 * gz + 80 * gx, 80, 80), f_send, f_recv
    )
    onward = {1: (5, 6, 4), 2: (8, 7), 3: (9,), 5: (10,), 6: (12, 11), 8: (13,), 12: (14,)}

    def forward(gather, number):
        gather.wait(number)
        gather.start(*onward[number])

    for number in onward:
        ops["A%d" % number] = functools.partial(forward, gather_a, number)
        ops["F%d" % number] = functools.partial(forward, gather_f, number)
    ops["Ax"] = functools.partial(gather_a.start, 1)

    def g_slot(gy, gx):
        return aligned(160 * (4 * gx + gy), 160, 160)

    def d_copy(number, rows, device, src=None):
        block = g_buf.at[rows]
        return remote(block if src is None else src, block, d_send, d_recv, number, device)

    d = [
        d_copy(0, g_slot(y, xlo), to_yp, grad),
        d_copy(1, g_slot(y, xlo), to_ym, grad),
        d_copy(2, g_slot(y, xlo), to_xlo, grad),
        d_copy(3, aligned(160 * (4 * xlo + ym), 80, 80), to_yp),
        d_copy(4, g_slot(ym, xlo), to_xlo),
        d_copy(5, aligned(160 * (4 * xlo + yp) + 80, 80, 80), to_ym),
        d_copy(6, g_slot(yp, xlo), to_xlo),
        d_copy(7, g_slot(y2, xlo), to_xlo),
        remote(g_buf.at[aligned(640 * (1 - core), 640, 640)], g_twin, d_send, d_recv, 8, to_core),
        remote(basis_out, bo_twin, d_send, d_recv, 9, to_core),
    ]

    def gradients_a():
        d[0].wait_recv()
        d[3].start()

    def gradients_b():
        d[1].wait_recv()
        d[5].start()

    def gradients_across(number):
        if number == 7:
            d[3].wait_recv()
            d[5].wait_recv()
        d[number].start()

    def gradients_x():
        for number in (2, 4, 6, 7):
            d[number].wait_recv()
        loads["grad"].wait()
        d[8].start()

    ops.update(Da=gradients_a, Db=gradients_b, Dx=gradients_x)
    for number in (2, 4, 6, 7):
        ops["Dc%d" % number] = functools.partial(gradients_across, number)

    def e_rows(ez):
        return aligned(160 * ez, 160, 160)

    left, right = pl.ds(0, 512), pl.ds(512, 512)
    e = [
        remote(part_out.at[e_rows(z2), left], land_z.at[0], e_send, e_recv, 0, to_zp),
        remote(part_out.at[e_rows(z2), right], land_z.at[1], e_send, e_recv, 1, to_zm),
        remote(part_out.at[e_rows(zm), left], land_z.at[2], e_send, e_recv, 2, to_zm),
        remote(part_out.at[e_rows(zp), right], land_z.at[3], e_send, e_recv, 3, to_zp),
        remote(part_out.at[e_rows(zp), left], land_z.at[4], e_send, e_recv, 4, to_zp),
        remote(part_out.at[e_rows(zm), right], land_z.at[5], e_send, e_recv, 5, to_zm),
        remote(part_out.at[aligned(160 * z + 80 * (1 - xhi), 80, 80)], land_h, e_send, e_recv, 6, to_xhi),
    ]

    def out_matmul():
        loads["basis_out"].wait()
        d[8].wait_recv()
        d[9].wait_recv()

        @pl.loop(0, 4)
        def _(n):
            rows = aligned(160 * n, 160, 160)
            part_out[rows, :] = jnp.dot(
                g_buf[aligned(640 * core + 160 * n, 160, 160), :], bo_buf[...], preferred_element_type=F32
            ) + jnp.dot(g_twin[rows, :], bo_twin[...], preferred_element_type=F32)

        for copy in e[:4]:
            copy.start()

    def out_a():
        e[0].wait_recv()
        part_out[e_rows(zp), left] += land_z[0]
        e[4].start()

    def out_b():
        e[1].wait_recv()
        part_out[e_rows(zm), right] += land_z[1]
        e[5].start()

    def out_sum():
        for copy in e[2:6]:
            copy.wait_recv()
        part_out[e_rows(z), left] += land_z[4] + land_z[2]
        part_out[e_rows(z), right] += land_z[5] + land_z[3]
        e[6].start()

    def out_final():
        e[6].wait_recv()
        rot_out[aligned(640 * core + 160 * z + 80 * xhi, 80, 80), :] = (
            part_out[aligned(160 * z + 80 * xhi, 80, 80), :] + land_h[...]
        ).astype(BF16)
        gather_f.start(1, 2, 3, 0)

    def out_done():
        gather_f.wait(0, 4, 7, 9, 10, 11, 13, 14)

    ops.update(outmm=out_matmul, outa=out_a, outb=out_b, outsum=out_sum, outfin=out_final, Fdone=out_done)

    class Unit:
        def __init__(self, u):
            self.u, self.slot = u, u % SLOTS
            if u < 2:
                self.start = 160 * (2 * z + (xhi, 1 - xhi)[u])
                self.need = ((0,), (4,))[u]
            else:
                self.start = 320 * (zm, zp, z2)[(u - 2) % 3]
                self.need = ((7, 10), (9, 11), (13, 14))[(u - 2) % 3]
            big, small = pl.ds(0, 48), pl.ds(48, 32)
            self.h = (big, small)
            if u % 2 == 0:
                self.up, self.down, to_up, to_down = yp, ym, to_yp, to_ym
                onward_a, onward_b = (48, 32), (0, 48)
            else:
                self.up, self.down, to_up, to_down = ym, yp, to_ym, to_yp
                onward_a, onward_b = (0, 48), (48, 32)

            def term(number, owner, rows, where, device):
                return remote(
                    send.at[u, owner, rows], land.at[u, where, rows], u_send.at[u], u_recv.at[u], number, device
                )

            def spread(number, owner, device, offset=0, count=80, piece=0):
                block = rot_in.at[self.place(owner, offset, count, piece)]
                return remote(block, block, u_send.at[u], u_recv.at[u], number, device)

            self.copies = [
                term(0, y2, big, 0, to_up),
                term(1, y2, small, 0, to_down),
                term(2, self.down, big, 1, to_down),
                term(3, self.up, small, 1, to_up),
                term(4, self.up, big, 2, to_up),
                term(5, self.down, small, 2, to_down),
                remote(send.at[u, y], land.at[u, 3], u_send.at[u], u_recv.at[u], 6, to_xlo),
            ]
            self.pieces = 2 if u >= 5 else 1
            for piece in range(self.pieces):
                number = 7 + 4 * piece
                self.copies += [
                    spread(number, y, to_yp, piece=piece),
                    spread(number + 1, y, to_ym, piece=piece),
                    spread(number + 2, ym, to_yp, *onward_a, piece=piece),
                    spread(number + 3, yp, to_ym, *onward_b, piece=piece),
                ]

        def place(self, owner, offset=0, count=80, piece=None):
            if self.u < 2:
                rows = aligned(self.start + 80 * (owner // 2) + offset, 16, count)
                return rows, aligned(HALF * lax.rem(owner, 2), 128, HALF)
            rows = aligned(self.start + 80 * owner + offset, 16, count)
            if self.u < 5:
                return rows, pl.ds(0, HALF)
            return rows, (pl.ds(HALF, HALF), pl.ds(HALF, 384), pl.ds(HALF + 384, 512))[0 if piece is None else 1 + piece]

        def matmul(self):
            if self.u == 0:
                loads["act"].wait()
                loads["basis_in"].wait()
            gather_a.wait(*[number for number in self.need if number not in arrived])
            arrived.update(self.need)
            if self.u < 2:
                rows = aligned(self.start, 160, 160)

                @pl.loop(0, 2)
                def _(n):
                    block = jnp.dot(
                        a_buf[rows, :], b_buf[:, aligned(HALF * n, HALF, HALF)], preferred_element_type=F32
                    )
                    for half in range(2):
                        piece = block[80 * half:80 * half + 80]
                        part[self.slot, 2 * half + n] = piece
                        send[self.u, 2 * half + n] = piece.astype(BF16)
            else:
                block = jnp.dot(
                    a_buf[aligned(self.start, 320, 320), :],
                    b_buf[:, HALF * ((self.u - 2) // 3):HALF * ((self.u - 2) // 3) + HALF],
                    preferred_element_type=F32,
                )
                for owner in range(4):
                    piece = block[80 * owner:80 * owner + 80]
                    part[self.slot, owner] = piece
                    send[self.u, owner] = piece.astype(BF16)
            for copy in self.copies[:4]:
                copy.start()

        def second(self, number):
            owner, rows = ((self.up, self.h[0]), (self.down, self.h[1]))[number]
            self.copies[number].wait_recv()
            send[self.u, owner, rows] = (
                part[self.slot, owner, rows] + land[self.u, 0, rows].astype(F32)
            ).astype(BF16)
            self.copies[4 + number].start()

        def third(self):
            for number in (2, 3, 4, 5):
                self.copies[number].wait_recv()
            total = part[self.slot, y] + (land[self.u, 1].astype(F32) + land[self.u, 2].astype(F32))
            part[self.slot, y] = total
            send[self.u, y] = total.astype(BF16)
            self.copies[6].start()

        def fourth(self):
            self.copies[6].wait_recv()
            rot_in[self.place(y)] = (part[self.slot, y] + land[self.u, 3].astype(F32)).astype(BF16)
            self.give(0)

        def give(self, piece):
            self.copies[7 + 4 * piece].start()
            self.copies[8 + 4 * piece].start()

        def spread_on(self, piece, number):
            self.copies[7 + 4 * piece + number].wait_recv()
            self.copies[9 + 4 * piece + number].start()

        def last(self, piece):
            self.copies[9 + 4 * piece].wait_recv()
            self.copies[10 + 4 * piece].wait_recv()

    arrived = set()
    units = [Unit(u) for u in range(8)]
    for u, unit in enumerate(units):
        ops["mm%d" % u] = unit.matmul
        ops["sa%d" % u] = functools.partial(unit.second, 0)
        ops["sb%d" % u] = functools.partial(unit.second, 1)
        ops["th%d" % u] = unit.third
        ops["fo%d" % u] = unit.fourth
        for piece in range(unit.pieces):
            ops["fg"[piece] + "a%d" % u] = functools.partial(unit.spread_on, piece, 0)
            ops["fg"[piece] + "b%d" % u] = functools.partial(unit.spread_on, piece, 1)
            ops["lk"[piece] + "a%d" % u] = functools.partial(unit.last, piece)
        if unit.pieces == 2:
            ops["go%d" % u] = functools.partial(unit.give, 1)

    def reciprocal():
        loads["eigen"].wait()

        @pl.loop(0, 16)
        def _(n):
            rows = aligned(64 * n, 64, 64)
            eig[rows, :] = 1.0 / eig[rows, :]

    def prepare():
        gather_a.finish()

        @pl.loop(0, 4)
        def _(n):
            rows = aligned(256 * n, 256, 256)
            turned = rot_out[:, rows].astype(F32).T
            for p, (first, last, at) in enumerate(WINDOWS):
                kept = jnp.where(ids[0:1, first:last] == p, turned[:, first:last], 0.0)
                a_buf[rows, at:at + last - first] = kept.astype(BF16)
            a_buf[rows, QUERY_AT:QUERY_AT + 256] = turned[:, 1024:1280].astype(BF16)

        acc[...] = jnp.zeros_like(acc)

    def final(chunks):
        @pl.loop(0, 2)
        def _(n):
            rows = aligned(512 * n, 512, 512)
            query = a_buf[rows, QUERY_AT:QUERY_AT + 256].astype(F32)
            for chunk in chunks:
                cols = slice(256 * chunk, 256 * chunk + 256)
                inverse = eig[rows, cols]
                scaled = []
                for first, last, at in WINDOWS:
                    pair_block = jnp.dot(
                        a_buf[rows, at:at + last - first], rot_in[first:last, cols], preferred_element_type=F32
                    )
                    scaled.append((pair_block * inverse).astype(BF16))
                mapped = lax.dot_general(
                    jnp.concatenate(scaled, axis=0),
                    rot_in[1024:1280, cols],
                    (((1,), (1,)), ((), ())),
                    preferred_element_type=F32,
                )
                for p in range(PAIRS):
                    product = mapped[512 * p:512 * p + 512] * query
                    acc[8 * p:8 * p + 8, :] += jnp.sum(product.reshape(64, 8, 256), axis=0)

    ops.update(rcp=reciprocal, prep=prepare)
    for number, chunks in enumerate(((0, 1, 2), (3, 4), (5, 6))):
        ops["fin%d" % number] = functools.partial(final, chunks)

    gather_a.start(2, 3, 0)
    d[0].start()
    d[1].start()
    d[9].start()
    for names in ORDER:
        for name in names:
            ops[name]()

    token = lax.broadcasted_iota(jnp.int32, (256, 128), 0)
    query = lax.broadcasted_iota(jnp.int32, (256, 128), 1)
    pick = jnp.where(token // QLEN == query, 1.0, 0.0)
    per_token = jnp.sum(acc[...].reshape(PAIRS, 8, 256), axis=1)
    red_row[row] = jnp.zeros((8, 128), F32)
    red_row[row, :PAIRS] = jnp.dot(per_token, pick, precision=lax.Precision.HIGHEST, preferred_element_type=F32)

    def everyone(red, position, mates, sends, recvs):
        copies = []
        for k, mate in enumerate(mates):
            copies.append(remote(red.at[position], red.at[position], sends, recvs, k, mate))
        for copy in copies:
            copy.start()
        for copy in copies:
            copy.wait_recv()
        return copies

    row_copies = everyone(red_row, row, row_mates, r_send, r_recv)
    red_col[col] = jnp.sum(red_row[...], axis=0)
    col_copies = everyone(red_col, col, col_mates, c_send, c_recv)
    scores[...] = jnp.sum(red_col[...], axis=0)[:PAIRS, :64]

    gather_f.finish()
    for copy in d + e + row_copies + col_copies:
        copy.wait_send()
    for unit in units:
        for copy in unit.copies:
            copy.wait_send()


def on_device(activations, gradients, basis_in, basis_out, eigen_damped, pair_ids):
    anywhere = pl.BlockSpec(memory_space=pl.ANY)
    vmem = pl.BlockSpec(memory_space=pltpu.VMEM)
    dma = pltpu.SemaphoreType.DMA
    return pl.pallas_call(
        kernel,
        out_shape=jax.ShapeDtypeStruct((PAIRS, 64), F32),
        in_specs=[anywhere] * 5 + [vmem],
        out_specs=vmem,
        scratch_shapes=[
            pltpu.VMEM((1280, 3584), BF16),
            pltpu.VMEM((3584, 1792), BF16),
            pltpu.VMEM((SLOTS, 4, 80, HALF), F32),
            pltpu.VMEM((8, 4, 80, HALF), BF16),
            pltpu.VMEM((8, 4, 80, HALF), BF16),
            pltpu.VMEM((1280, 1792), BF16),
            pltpu.VMEM((1280, 512), BF16),
            pltpu.VMEM((640, 512), BF16),
            pltpu.VMEM((512, 1024), BF16),
            pltpu.VMEM((512, 1024), BF16),
            pltpu.VMEM((640, 1024), F32),
            pltpu.VMEM((6, 160, 512), F32),
            pltpu.VMEM((80, 1024), F32),
            pltpu.VMEM((1280, 1024), BF16),
            pltpu.VMEM((1024, 1792), F32),
            pltpu.VMEM((8 * PAIRS, 256), F32),
            pltpu.VMEM((8, 8, 128), F32),
            pltpu.VMEM((16, 8, 128), F32),
            dma((15,)), dma((15,)),
            dma((10,)), dma((10,)),
            dma((7,)), dma((7,)),
            dma((15,)), dma((15,)),
            dma((8, 15)), dma((8, 15)),
            dma((7,)), dma((7,)),
            dma((15,)), dma((15,)),
            dma((5,)),
        ],
        compiler_params=pltpu.CompilerParams(
            collective_id=0, has_side_effects=True, vmem_limit_bytes=63 * 2**20
        ),
        cost_estimate=pl.CostEstimate(flops=28 * 10**9, bytes_accessed=22 * 10**6, transcendentals=0),
    )(activations, gradients, basis_in, basis_out, eigen_damped, pair_ids.reshape(1, 1024))


def solution(mesh):
    return jax.shard_map(
        on_device,
        mesh=mesh,
        in_specs=(
            P("col", "row"),
            P("row", "col"),
            P("row", "col"),
            P("col", "row"),
            P("row", "col"),
            P(),
        ),
        out_specs=P(),
        check_vma=False,
    )
```

```python
import functools

import jax
import jax.numpy as jnp
from jax import lax
from jax.experimental import pallas as pl
from jax.experimental.pallas import tpu as pltpu
from jax.sharding import PartitionSpec as P

PAIRS = 4
QLEN = 4
WINDOWS = ((0, 384, 0), (0, 768, 384), (256, 1024, 1152), (640, 1024, 1920))
QUERY_AT = 2304
HALF = 896
SLOTS = 5
MESH = pl.DeviceIdType.MESH
BF16 = jnp.bfloat16
F32 = jnp.float32


def aligned(start, multiple, size):
    return pl.ds(pl.multiple_of(start, multiple), size)


class Place:
    def __init__(self):
        row, col = lax.axis_index("row"), lax.axis_index("col")
        self.xlo, self.y = row // 4, lax.rem(row, 4)
        self.z, self.xhi, self.core = col // 4, lax.rem(col // 2, 2), lax.rem(col, 2)

    def at(self, xlo=None, y=None, z=None, xhi=None, core=None):
        xlo = self.xlo if xlo is None else xlo
        y = self.y if y is None else y
        z = self.z if z is None else z
        xhi = self.xhi if xhi is None else xhi
        core = self.core if core is None else core
        return (xlo * 4 + y, z * 4 + xhi * 2 + core)


def remote(src, dst, sends, recvs, number, device):
    return pltpu.make_async_remote_copy(
        src_ref=src,
        dst_ref=dst,
        send_sem=sends.at[number],
        recv_sem=recvs.at[number],
        device_id=device,
        device_id_type=MESH,
    )


class Gather:
    def __init__(self, place, buf, slot, sends, recvs, first=None):
        zp, zm, z2 = (lax.rem(place.z + k, 4) for k in (1, 3, 2))
        xhi, other = place.xhi, 1 - place.xhi
        core, twin = place.core, 1 - place.core
        to_core, to_xhi = place.at(core=twin), place.at(xhi=other)
        to_zp, to_zm = place.at(z=zp), place.at(z=zm)
        z = place.z
        plan = [
            (z, xhi, to_core), (z, xhi, to_xhi), (z, xhi, to_zp), (z, xhi, to_zm),
            (z, other, to_core), (z, other, to_zp), (z, other, to_zm),
            (zm, xhi, to_core), (zm, xhi, to_zp), (zp, xhi, to_core),
            (zm, other, to_core), (zp, other, to_core), (zp, other, to_zm),
            (z2, xhi, to_core), (z2, other, to_core),
        ]
        self.copies = []
        for number, (from_z, from_x, device) in enumerate(plan):
            block = buf.at[slot(from_z, from_x, core)]
            src = first if number < 4 and first is not None else block
            self.copies.append(remote(src, block, sends, recvs, number, device))

    def start(self, *numbers):
        for number in numbers:
            self.copies[number].start()

    def wait(self, *numbers):
        for number in numbers:
            self.copies[number].wait_recv()

    def finish(self):
        for copy in self.copies:
            copy.wait_send()


ORDER = (
    ("Ax", "mm0", "Dc2", "Da", "sb0", "Db", "sa0", "A1", "A3", "th0", "Dc7", "A2", "Dc6", "mm1", "fo0", "mm3"),
    ("mm2", "Dc4", "A6", "sb1", "fa0", "sa1", "A5", "fb0", "mm5", "Dx", "sa3", "sb3", "sb2", "mm4", "outmm0"),
    ("la0", "sa2", "th1", "sa4", "sa5", "th3", "outmm1", "rcp", "A8", "sb5", "outa0", "A12", "th2", "fo1", "sb4"),
    ("fo3", "th5", "mm6", "outb0", "fo2", "outb1", "th4", "fa1", "mm7", "sa6", "outa1", "sb6", "outsum0", "fb2"),
    ("outsum1", "sb7", "outfin0", "fb1", "fa3", "fo5", "th6", "outfin1", "sa7", "fo4", "H2", "F3", "F1", "la1"),
    ("H1", "fo6", "H8", "fb5", "H3", "fa5", "th7", "fa2", "fb3", "F2", "H6", "fb6", "F6", "fo7", "fa6", "H12"),
    ("la3", "F8", "F5", "la5", "H5", "fb4", "la2", "F12", "fa4", "go7", "fa7", "fb7", "la6", "Fdone", "prep"),
    ("la4", "fin0", "gb7", "la7", "ga7", "fin1", "ka7", "fin2"),
)


def kernel(
    act, grad, basis_in, basis_out, eigen, ids, scores,
    a_buf, b_buf, part, send, land, rot_in,
    g_buf, g_twin, bo_buf, bo_twin, part_out, land_z, land_h, rot_out,
    eig, acc, red_row, red_col,
    a_send, a_recv, d_send, d_recv, e_send, e_recv, f_send, f_recv, u_send, u_recv,
    r_send, r_recv, c_send, c_recv, local,
):
    me = Place()
    row, col = lax.axis_index("row"), lax.axis_index("col")
    xlo, y, z, xhi, core = me.xlo, me.y, me.z, me.xhi, me.core
    yp, ym, y2 = (lax.rem(y + k, 4) for k in (1, 3, 2))
    zp, zm, z2 = (lax.rem(z + k, 4) for k in (1, 3, 2))
    to_yp, to_ym = me.at(y=yp), me.at(y=ym)
    to_zp, to_zm = me.at(z=zp), me.at(z=zm)
    to_xlo, to_xhi, to_core = me.at(xlo=1 - xlo), me.at(xhi=1 - xhi), me.at(core=1 - core)
    row_mates = [(lax.rem(row + k, 8), col) for k in range(1, 8)]
    col_mates = [(row, lax.rem(col + k, 16)) for k in range(1, 16)]

    loads = {
        "act": pltpu.make_async_copy(act, a_buf.at[aligned(80 * (4 * z + 2 * xhi + core), 80, 80)], local.at[0]),
        "grad": pltpu.make_async_copy(grad, g_buf.at[aligned(160 * (4 * xlo + y), 160, 160)], local.at[1]),
        "basis_in_0": pltpu.make_async_copy(basis_in.at[:, pl.ds(0, HALF)], b_buf.at[:, pl.ds(0, HALF)], local.at[2]),
        "basis_in_1": pltpu.make_async_copy(basis_in.at[:, pl.ds(HALF, HALF)], b_buf.at[:, pl.ds(HALF, HALF)], local.at[5]),
        "basis_out": pltpu.make_async_copy(basis_out, bo_buf, local.at[3]),
        "eigen": pltpu.make_async_copy(eigen, eig, local.at[4]),
    }
    barrier = pltpu.get_barrier_semaphore()
    for mate in row_mates + col_mates:
        pl.semaphore_signal(barrier, inc=1, device_id=mate, device_id_type=MESH)
    pl.semaphore_wait(barrier, len(row_mates) + len(col_mates))

    ops = {}

    gather_a = Gather(
        me, a_buf, lambda gz, gx, gc: aligned(80 * (4 * gz + 2 * gx + gc), 80, 80), a_send, a_recv, act
    )
    gather_out = [
        Gather(
            me, rot_out.at[:, pl.ds(512 * lane, 512)],
            lambda gz, gx, gc: aligned(640 * gc + 160 * gz + 80 * gx, 80, 80), f_send.at[lane], f_recv.at[lane],
        )
        for lane in range(2)
    ]
    onward = {1: (5, 6, 4), 2: (8, 7), 3: (9,), 5: (10,), 6: (12, 11), 8: (13,), 12: (14,)}

    def forward(gather, number):
        gather.wait(number)
        gather.start(*onward[number])

    for number in onward:
        ops["A%d" % number] = functools.partial(forward, gather_a, number)
        ops["F%d" % number] = functools.partial(forward, gather_out[0], number)
        ops["H%d" % number] = functools.partial(forward, gather_out[1], number)
    ops["Ax"] = functools.partial(gather_a.start, 1)

    def g_slot(gy, gx):
        return aligned(160 * (4 * gx + gy), 160, 160)

    def d_copy(number, rows, device, src=None):
        block = g_buf.at[rows]
        return remote(block if src is None else src, block, d_send, d_recv, number, device)

    d = [
        d_copy(0, g_slot(y, xlo), to_yp, grad),
        d_copy(1, g_slot(y, xlo), to_ym, grad),
        d_copy(2, g_slot(y, xlo), to_xlo, grad),
        d_copy(3, aligned(160 * (4 * xlo + ym), 80, 80), to_yp),
        d_copy(4, g_slot(ym, xlo), to_xlo),
        d_copy(5, aligned(160 * (4 * xlo + yp) + 80, 80, 80), to_ym),
        d_copy(6, g_slot(yp, xlo), to_xlo),
        d_copy(7, g_slot(y2, xlo), to_xlo),
        remote(g_buf.at[aligned(640 * (1 - core), 640, 640)], g_twin, d_send, d_recv, 8, to_core),
        remote(basis_out, bo_twin, d_send, d_recv, 9, to_core),
    ]

    def gradients_a():
        d[0].wait_recv()
        d[3].start()

    def gradients_b():
        d[1].wait_recv()
        d[5].start()

    def gradients_across(number):
        if number == 7:
            d[3].wait_recv()
            d[5].wait_recv()
        d[number].start()

    def gradients_x():
        for number in (2, 4, 6, 7):
            d[number].wait_recv()
        loads["grad"].wait()
        d[8].start()

    ops.update(Da=gradients_a, Db=gradients_b, Dx=gradients_x)
    for number in (2, 4, 6, 7):
        ops["Dc%d" % number] = functools.partial(gradients_across, number)

    def e_rows(ez):
        return aligned(160 * ez, 160, 160)

    class Lane:
        def __init__(self, lane):
            self.lane, self.cols = lane, pl.ds(512 * lane, 512)
            self.left, self.right = pl.ds(512 * lane, 256), pl.ds(512 * lane + 256, 256)

            def term(number, ez, cols, device):
                return remote(
                    part_out.at[e_rows(ez), cols], land_z.at[lane, number], e_send.at[lane], e_recv.at[lane], number, device
                )

            self.e = [
                term(0, z2, self.left, to_zp),
                term(1, z2, self.right, to_zm),
                term(2, zm, self.left, to_zm),
                term(3, zp, self.right, to_zp),
                term(4, zp, self.left, to_zp),
                term(5, zm, self.right, to_zm),
                remote(
                    part_out.at[aligned(160 * z + 80 * (1 - xhi), 80, 80), self.cols],
                    land_h.at[lane], e_send.at[lane], e_recv.at[lane], 6, to_xhi,
                ),
            ]

        def matmul(self):
            if self.lane == 0:
                loads["basis_out"].wait()
                d[8].wait_recv()
                d[9].wait_recv()

            @pl.loop(0, 2)
            def _(n):
                rows = aligned(320 * n, 320, 320)
                part_out[rows, self.cols] = jnp.dot(
                    g_buf[aligned(640 * core + 320 * n, 320, 320), :], bo_buf[:, self.cols], preferred_element_type=F32
                ) + jnp.dot(g_twin[rows, :], bo_twin[:, self.cols], preferred_element_type=F32)

            for copy in self.e[:4]:
                copy.start()

        def second_a(self):
            self.e[0].wait_recv()
            part_out[e_rows(zp), self.left] += land_z[self.lane, 0]
            self.e[4].start()

        def second_b(self):
            self.e[1].wait_recv()
            part_out[e_rows(zm), self.right] += land_z[self.lane, 1]
            self.e[5].start()

        def total(self):
            for copy in self.e[2:6]:
                copy.wait_recv()
            part_out[e_rows(z), self.left] += land_z[self.lane, 4] + land_z[self.lane, 2]
            part_out[e_rows(z), self.right] += land_z[self.lane, 5] + land_z[self.lane, 3]
            self.e[6].start()

        def finish(self):
            self.e[6].wait_recv()
            rot_out[aligned(640 * core + 160 * z + 80 * xhi, 80, 80), self.cols] = (
                part_out[aligned(160 * z + 80 * xhi, 80, 80), self.cols] + land_h[self.lane]
            ).astype(BF16)
            gather_out[self.lane].start(1, 2, 3, 0)

    lanes = [Lane(0), Lane(1)]
    for lane in lanes:
        ops["outmm%d" % lane.lane] = lane.matmul
        ops["outa%d" % lane.lane] = lane.second_a
        ops["outb%d" % lane.lane] = lane.second_b
        ops["outsum%d" % lane.lane] = lane.total
        ops["outfin%d" % lane.lane] = lane.finish

    def out_done():
        for gather in gather_out:
            gather.wait(0, 4, 7, 9, 10, 11, 13, 14)

    ops["Fdone"] = out_done

    class Unit:
        def __init__(self, u):
            self.u, self.slot = u, u % SLOTS
            if u < 6:
                block_z, block_x = (z, z, zm, zp, zm, zp)[u], (xhi, 1 - xhi, xhi, xhi, 1 - xhi, 1 - xhi)[u]
                self.start = 160 * (2 * block_z + block_x)
                self.need = ((0,), (4,), (7,), (9,), (10,), (11,))[u]
            else:
                self.start = 320 * z2
                self.need = (13, 14)
            big, small = pl.ds(0, 48), pl.ds(48, 32)
            self.h = (big, small)
            if u % 2 == 0:
                self.up, self.down, to_up, to_down = yp, ym, to_yp, to_ym
                onward_a, onward_b = (48, 32), (0, 48)
            else:
                self.up, self.down, to_up, to_down = ym, yp, to_ym, to_yp
                onward_a, onward_b = (0, 48), (48, 32)

            def term(number, owner, rows, where, device):
                return remote(
                    send.at[u, owner, rows], land.at[u, where, rows], u_send.at[u], u_recv.at[u], number, device
                )

            def spread(number, owner, device, offset=0, count=80, piece=0):
                block = rot_in.at[self.place(owner, offset, count, piece)]
                return remote(block, block, u_send.at[u], u_recv.at[u], number, device)

            self.copies = [
                term(0, y2, big, 0, to_up),
                term(1, y2, small, 0, to_down),
                term(2, self.down, big, 1, to_down),
                term(3, self.up, small, 1, to_up),
                term(4, self.up, big, 2, to_up),
                term(5, self.down, small, 2, to_down),
                remote(send.at[u, y], land.at[u, 3], u_send.at[u], u_recv.at[u], 6, to_xlo),
            ]
            self.pieces = 2 if u == 7 else 1
            for piece in range(self.pieces):
                number = 7 + 4 * piece
                self.copies += [
                    spread(number, y, to_yp, piece=piece),
                    spread(number + 1, y, to_ym, piece=piece),
                    spread(number + 2, ym, to_yp, *onward_a, piece=piece),
                    spread(number + 3, yp, to_ym, *onward_b, piece=piece),
                ]

        def place(self, owner, offset=0, count=80, piece=None):
            if self.u < 6:
                rows = aligned(self.start + 80 * (owner // 2) + offset, 16, count)
                return rows, aligned(HALF * lax.rem(owner, 2), 128, HALF)
            rows = aligned(self.start + 80 * owner + offset, 16, count)
            if self.u == 6:
                return rows, pl.ds(0, HALF)
            return rows, (pl.ds(HALF, HALF), pl.ds(HALF, 384), pl.ds(HALF + 384, 512))[0 if piece is None else 1 + piece]

        def matmul(self):
            if self.u == 0:
                loads["act"].wait()
            gather_a.wait(*[number for number in self.need if number not in arrived])
            arrived.update(self.need)
            if self.u < 6:
                rows = aligned(self.start, 160, 160)

                def columns(n):
                    block = jnp.dot(
                        a_buf[rows, :], b_buf[:, aligned(HALF * n, HALF, HALF)], preferred_element_type=F32
                    )
                    for half in range(2):
                        piece = block[80 * half:80 * half + 80]
                        part[self.slot, 2 * half + n] = piece
                        send[self.u, 2 * half + n] = piece.astype(BF16)

                if self.u == 0:
                    loads["basis_in_0"].wait()
                    columns(0)
                    loads["basis_in_1"].wait()
                    columns(1)
                    loads["eigen"].start()
                else:
                    pl.loop(0, 2)(columns)
            else:
                block = jnp.dot(
                    a_buf[aligned(self.start, 320, 320), :],
                    b_buf[:, HALF * (self.u - 6):HALF * (self.u - 6) + HALF],
                    preferred_element_type=F32,
                )
                for owner in range(4):
                    piece = block[80 * owner:80 * owner + 80]
                    part[self.slot, owner] = piece
                    send[self.u, owner] = piece.astype(BF16)
            for copy in self.copies[:4]:
                copy.start()

        def second(self, number):
            owner, rows = ((self.up, self.h[0]), (self.down, self.h[1]))[number]
            self.copies[number].wait_recv()
            send[self.u, owner, rows] = (
                part[self.slot, owner, rows] + land[self.u, 0, rows].astype(F32)
            ).astype(BF16)
            self.copies[4 + number].start()

        def third(self):
            for number in (2, 3, 4, 5):
                self.copies[number].wait_recv()
            total = part[self.slot, y] + (land[self.u, 1].astype(F32) + land[self.u, 2].astype(F32))
            part[self.slot, y] = total
            send[self.u, y] = total.astype(BF16)
            self.copies[6].start()

        def fourth(self):
            self.copies[6].wait_recv()
            rot_in[self.place(y)] = (part[self.slot, y] + land[self.u, 3].astype(F32)).astype(BF16)
            self.give(0)

        def give(self, piece):
            self.copies[7 + 4 * piece].start()
            self.copies[8 + 4 * piece].start()

        def spread_on(self, piece, number):
            self.copies[7 + 4 * piece + number].wait_recv()
            self.copies[9 + 4 * piece + number].start()

        def last(self, piece):
            self.copies[9 + 4 * piece].wait_recv()
            self.copies[10 + 4 * piece].wait_recv()

    arrived = set()
    units = [Unit(u) for u in range(8)]
    for u, unit in enumerate(units):
        ops["mm%d" % u] = unit.matmul
        ops["sa%d" % u] = functools.partial(unit.second, 0)
        ops["sb%d" % u] = functools.partial(unit.second, 1)
        ops["th%d" % u] = unit.third
        ops["fo%d" % u] = unit.fourth
        for piece in range(unit.pieces):
            ops["fg"[piece] + "a%d" % u] = functools.partial(unit.spread_on, piece, 0)
            ops["fg"[piece] + "b%d" % u] = functools.partial(unit.spread_on, piece, 1)
            ops["lk"[piece] + "a%d" % u] = functools.partial(unit.last, piece)
        if unit.pieces == 2:
            ops["go%d" % u] = functools.partial(unit.give, 1)

    def reciprocal():
        loads["eigen"].wait()

        @pl.loop(0, 16)
        def _(n):
            rows = aligned(64 * n, 64, 64)
            eig[rows, :] = 1.0 / eig[rows, :]

    def prepare():
        gather_a.finish()

        @pl.loop(0, 4)
        def _(n):
            rows = aligned(256 * n, 256, 256)
            turned = rot_out[:, rows].astype(F32).T
            for p, (first, last, at) in enumerate(WINDOWS):
                kept = jnp.where(ids[0:1, first:last] == p, turned[:, first:last], 0.0)
                a_buf[rows, at:at + last - first] = kept.astype(BF16)
            a_buf[rows, QUERY_AT:QUERY_AT + 256] = turned[:, 1024:1280].astype(BF16)

        acc[...] = jnp.zeros_like(acc)

    def final(chunks):
        @pl.loop(0, 2)
        def _(n):
            rows = aligned(512 * n, 512, 512)
            query = a_buf[rows, QUERY_AT:QUERY_AT + 256].astype(F32)
            for chunk in chunks:
                cols = slice(256 * chunk, 256 * chunk + 256)
                inverse = eig[rows, cols]
                scaled = []
                for first, last, at in WINDOWS:
                    pair_block = jnp.dot(
                        a_buf[rows, at:at + last - first], rot_in[first:last, cols], preferred_element_type=F32
                    )
                    scaled.append((pair_block * inverse).astype(BF16))
                mapped = lax.dot_general(
                    jnp.concatenate(scaled, axis=0),
                    rot_in[1024:1280, cols],
                    (((1,), (1,)), ((), ())),
                    preferred_element_type=F32,
                )
                for p in range(PAIRS):
                    product = mapped[512 * p:512 * p + 512] * query
                    acc[8 * p:8 * p + 8, :] += jnp.sum(product.reshape(64, 8, 256), axis=0)

    ops.update(rcp=reciprocal, prep=prepare)
    for number, chunks in enumerate(((0, 1, 2), (3, 4), (5, 6))):
        ops["fin%d" % number] = functools.partial(final, chunks)

    gather_a.start(2, 3, 0)
    d[0].start()
    d[1].start()
    d[9].start()
    for name in ("act", "basis_in_0", "basis_in_1", "grad", "basis_out"):
        loads[name].start()
    for names in ORDER:
        for name in names:
            ops[name]()

    token = lax.broadcasted_iota(jnp.int32, (256, 128), 0)
    query = lax.broadcasted_iota(jnp.int32, (256, 128), 1)
    pick = jnp.where(token // QLEN == query, 1.0, 0.0)
    per_token = jnp.sum(acc[...].reshape(PAIRS, 8, 256), axis=1)
    red_row[row] = jnp.zeros((8, 128), F32)
    red_row[row, :PAIRS] = jnp.dot(per_token, pick, precision=lax.Precision.HIGHEST, preferred_element_type=F32)

    def everyone(red, position, mates, sends, recvs):
        copies = []
        for k, mate in enumerate(mates):
            copies.append(remote(red.at[position], red.at[position], sends, recvs, k, mate))
        for copy in copies:
            copy.start()
        for copy in copies:
            copy.wait_recv()
        return copies

    row_copies = everyone(red_row, row, row_mates, r_send, r_recv)
    red_col[col] = jnp.sum(red_row[...], axis=0)
    col_copies = everyone(red_col, col, col_mates, c_send, c_recv)
    scores[...] = jnp.sum(red_col[...], axis=0)[:PAIRS, :64]

    for gather in gather_out:
        gather.finish()
    for copy in d + lanes[0].e + lanes[1].e + row_copies + col_copies:
        copy.wait_send()
    for unit in units:
        for copy in unit.copies:
            copy.wait_send()


def on_device(activations, gradients, basis_in, basis_out, eigen_damped, pair_ids):
    anywhere = pl.BlockSpec(memory_space=pl.ANY)
    vmem = pl.BlockSpec(memory_space=pltpu.VMEM)
    dma = pltpu.SemaphoreType.DMA
    return pl.pallas_call(
        kernel,
        out_shape=jax.ShapeDtypeStruct((PAIRS, 64), F32),
        in_specs=[anywhere] * 5 + [vmem],
        out_specs=vmem,
        scratch_shapes=[
            pltpu.VMEM((1280, 3584), BF16),
            pltpu.VMEM((3584, 1792), BF16),
            pltpu.VMEM((SLOTS, 4, 80, HALF), F32),
            pltpu.VMEM((8, 4, 80, HALF), BF16),
            pltpu.VMEM((8, 4, 80, HALF), BF16),
            pltpu.VMEM((1280, 1792), BF16),
            pltpu.VMEM((1280, 512), BF16),
            pltpu.VMEM((640, 512), BF16),
            pltpu.VMEM((512, 1024), BF16),
            pltpu.VMEM((512, 1024), BF16),
            pltpu.VMEM((640, 1024), F32),
            pltpu.VMEM((2, 6, 160, 256), F32),
            pltpu.VMEM((2, 80, 512), F32),
            pltpu.VMEM((1280, 1024), BF16),
            pltpu.VMEM((1024, 1792), F32),
            pltpu.VMEM((8 * PAIRS, 256), F32),
            pltpu.VMEM((8, 8, 128), F32),
            pltpu.VMEM((16, 8, 128), F32),
            dma((15,)), dma((15,)),
            dma((10,)), dma((10,)),
            dma((2, 7)), dma((2, 7)),
            dma((2, 15)), dma((2, 15)),
            dma((8, 15)), dma((8, 15)),
            dma((7,)), dma((7,)),
            dma((15,)), dma((15,)),
            dma((6,)),
        ],
        compiler_params=pltpu.CompilerParams(
            collective_id=0, has_side_effects=True, vmem_limit_bytes=63 * 2**20
        ),
        cost_estimate=pl.CostEstimate(flops=28 * 10**9, bytes_accessed=22 * 10**6, transcendentals=0),
    )(activations, gradients, basis_in, basis_out, eigen_damped, pair_ids.reshape(1, 1024))


def solution(mesh):
    return jax.shard_map(
        on_device,
        mesh=mesh,
        in_specs=(
            P("col", "row"),
            P("row", "col"),
            P("row", "col"),
            P("col", "row"),
            P("row", "col"),
            P(),
        ),
        out_specs=P(),
        check_vma=False,
    )
```

```python
import functools

import jax
import jax.numpy as jnp
from jax import lax
from jax.experimental import pallas as pl
from jax.experimental.pallas import tpu as pltpu
from jax.sharding import PartitionSpec as P

PAIRS = 4
QLEN = 4
WINDOWS = ((0, 384, 0), (0, 768, 384), (256, 1024, 1152), (640, 1024, 1920))
QUERY_AT = 2304
HALF = 896
SLOTS = 5
MESH = pl.DeviceIdType.MESH
BF16 = jnp.bfloat16
F32 = jnp.float32


def aligned(start, multiple, size):
    return pl.ds(pl.multiple_of(start, multiple), size)


class Place:
    def __init__(self):
        row, col = lax.axis_index("row"), lax.axis_index("col")
        self.xlo, self.y = row // 4, lax.rem(row, 4)
        self.z, self.xhi, self.core = col // 4, lax.rem(col // 2, 2), lax.rem(col, 2)

    def at(self, xlo=None, y=None, z=None, xhi=None, core=None):
        xlo = self.xlo if xlo is None else xlo
        y = self.y if y is None else y
        z = self.z if z is None else z
        xhi = self.xhi if xhi is None else xhi
        core = self.core if core is None else core
        return (xlo * 4 + y, z * 4 + xhi * 2 + core)


def remote(src, dst, sends, recvs, number, device):
    return pltpu.make_async_remote_copy(
        src_ref=src,
        dst_ref=dst,
        send_sem=sends.at[number],
        recv_sem=recvs.at[number],
        device_id=device,
        device_id_type=MESH,
    )


class Gather:
    def __init__(self, place, buf, slot, sends, recvs, first=None):
        zp, zm, z2 = (lax.rem(place.z + k, 4) for k in (1, 3, 2))
        xhi, other = place.xhi, 1 - place.xhi
        core, twin = place.core, 1 - place.core
        to_core, to_xhi = place.at(core=twin), place.at(xhi=other)
        to_zp, to_zm = place.at(z=zp), place.at(z=zm)
        z = place.z
        plan = [
            (z, xhi, to_core), (z, xhi, to_xhi), (z, xhi, to_zp), (z, xhi, to_zm),
            (z, other, to_core), (z, other, to_zp), (z, other, to_zm),
            (zm, xhi, to_core), (zm, xhi, to_zp), (zp, xhi, to_core),
            (zm, other, to_core), (zp, other, to_core), (zp, other, to_zm),
            (z2, xhi, to_core), (z2, other, to_core),
        ]
        self.copies = []
        for number, (from_z, from_x, device) in enumerate(plan):
            block = buf.at[slot(from_z, from_x, core)]
            src = first if number < 4 and first is not None else block
            self.copies.append(remote(src, block, sends, recvs, number, device))

    def start(self, *numbers):
        for number in numbers:
            self.copies[number].start()

    def wait(self, *numbers):
        for number in numbers:
            self.copies[number].wait_recv()

    def finish(self):
        for copy in self.copies:
            copy.wait_send()


ORDER = (
    ("Ax", "mm0", "Da", "Dc2", "sa0", "sb0", "A3", "A1", "th0", "Dc4", "Db", "mm3", "fo0", "A2", "mm1", "Dc7"),
    ("mm2", "A5", "sb3", "A6", "sa3", "Dc6", "sa1", "rcp", "sb1", "mm4", "sa2", "Dx", "sb2", "mm5", "outmm0"),
    ("sb4", "A8", "th1", "A12", "sa4", "sb5", "sa5", "th3", "th2", "outb0", "fo1", "outa0", "mm6", "th5", "fo3"),
    ("outmm1", "fo2", "fb0", "outsum0", "sb6", "fa0", "outb1", "sa6", "th4", "outa1", "mm7", "outfin0", "fb2"),
    ("fo4", "fb1", "fa2", "fa1", "fb3", "outsum1", "sb7", "th6", "F1", "fa3", "F3", "sa7", "F6", "la0", "outfin1"),
    ("fa4", "fb4", "F2", "fo5", "la1", "fo6", "go5", "H1", "F12", "th7", "H2", "H6", "H5", "fo7", "la3", "H3"),
    ("fa6", "fb6", "la2", "F8", "fb5", "H12", "F5", "go7", "H8", "Fdone", "fa5", "gb5", "la4", "prep", "ga5"),
    ("fb7", "fa7", "la6", "fin0", "ga7", "la5", "la7", "gb7", "ka5", "fin1", "ka7", "fin2"),
)


def kernel(
    act, grad, basis_in, basis_out, eigen, ids, scores,
    a_buf, b_buf, part, send, land, rot_in,
    g_buf, g_twin, bo_buf, bo_twin, part_out, land_z, land_h, rot_out,
    eig, acc, red_row, red_col,
    a_send, a_recv, d_send, d_recv, e_send, e_recv, f_send, f_recv, u_send, u_recv,
    r_send, r_recv, c_send, c_recv, local,
):
    me = Place()
    row, col = lax.axis_index("row"), lax.axis_index("col")
    xlo, y, z, xhi, core = me.xlo, me.y, me.z, me.xhi, me.core
    yp, ym, y2 = (lax.rem(y + k, 4) for k in (1, 3, 2))
    zp, zm, z2 = (lax.rem(z + k, 4) for k in (1, 3, 2))
    to_yp, to_ym = me.at(y=yp), me.at(y=ym)
    to_zp, to_zm = me.at(z=zp), me.at(z=zm)
    to_xlo, to_xhi, to_core = me.at(xlo=1 - xlo), me.at(xhi=1 - xhi), me.at(core=1 - core)
    row_mates = [(lax.rem(row + k, 8), col) for k in range(1, 8)]
    col_mates = [(row, lax.rem(col + k, 16)) for k in range(1, 16)]

    loads = {
        "act": pltpu.make_async_copy(act, a_buf.at[aligned(80 * (4 * z + 2 * xhi + core), 80, 80)], local.at[0]),
        "grad": pltpu.make_async_copy(grad, g_buf.at[aligned(160 * (4 * xlo + y), 160, 160)], local.at[1]),
        "basis_in_0": pltpu.make_async_copy(basis_in.at[:, pl.ds(0, HALF)], b_buf.at[:, pl.ds(0, HALF)], local.at[2]),
        "basis_in_1": pltpu.make_async_copy(basis_in.at[:, pl.ds(HALF, HALF)], b_buf.at[:, pl.ds(HALF, HALF)], local.at[5]),
        "basis_out": pltpu.make_async_copy(basis_out, bo_buf, local.at[3]),
        "eigen": pltpu.make_async_copy(eigen, eig, local.at[4]),
    }
    barrier = pltpu.get_barrier_semaphore()
    friends = (to_yp, to_ym, to_zp, to_zm, to_xlo, to_xhi, to_core)
    for friend in friends:
        pl.semaphore_signal(barrier, inc=1, device_id=friend, device_id_type=MESH)
    pl.semaphore_wait(barrier, len(friends))

    ops = {}

    gather_a = Gather(
        me, a_buf, lambda gz, gx, gc: aligned(80 * (4 * gz + 2 * gx + gc), 80, 80), a_send, a_recv, act
    )
    gather_out = [
        Gather(
            me, rot_out.at[:, pl.ds(512 * lane, 512)],
            lambda gz, gx, gc: aligned(640 * gc + 160 * gz + 80 * gx, 80, 80), f_send.at[lane], f_recv.at[lane],
        )
        for lane in range(2)
    ]
    onward = {1: (5, 6, 4), 2: (8, 7), 3: (9,), 5: (10,), 6: (12, 11), 8: (13,), 12: (14,)}

    def forward(gather, number):
        gather.wait(number)
        gather.start(*onward[number])

    for number in onward:
        ops["A%d" % number] = functools.partial(forward, gather_a, number)
        ops["F%d" % number] = functools.partial(forward, gather_out[0], number)
        ops["H%d" % number] = functools.partial(forward, gather_out[1], number)
    ops["Ax"] = functools.partial(gather_a.start, 1)

    def g_slot(gy, gx):
        return aligned(160 * (4 * gx + gy), 160, 160)

    def d_copy(number, rows, device, src=None):
        block = g_buf.at[rows]
        return remote(block if src is None else src, block, d_send, d_recv, number, device)

    d = [
        d_copy(0, g_slot(y, xlo), to_yp, grad),
        d_copy(1, g_slot(y, xlo), to_ym, grad),
        d_copy(2, g_slot(y, xlo), to_xlo, grad),
        d_copy(3, aligned(160 * (4 * xlo + ym), 80, 80), to_yp),
        d_copy(4, g_slot(ym, xlo), to_xlo),
        d_copy(5, aligned(160 * (4 * xlo + yp) + 80, 80, 80), to_ym),
        d_copy(6, g_slot(yp, xlo), to_xlo),
        d_copy(7, g_slot(y2, xlo), to_xlo),
        remote(g_buf.at[aligned(640 * (1 - core), 640, 640)], g_twin, d_send, d_recv, 8, to_core),
        remote(basis_out, bo_twin, d_send, d_recv, 9, to_core),
    ]

    def gradients_a():
        d[0].wait_recv()
        d[3].start()

    def gradients_b():
        d[1].wait_recv()
        d[5].start()

    def gradients_across(number):
        if number == 7:
            d[3].wait_recv()
            d[5].wait_recv()
        d[number].start()

    def gradients_x():
        for number in (2, 4, 6, 7):
            d[number].wait_recv()
        loads["grad"].wait()
        d[8].start()

    ops.update(Da=gradients_a, Db=gradients_b, Dx=gradients_x)
    for number in (2, 4, 6, 7):
        ops["Dc%d" % number] = functools.partial(gradients_across, number)

    def e_rows(ez):
        return aligned(160 * ez, 160, 160)

    class Lane:
        def __init__(self, lane):
            self.lane, self.cols = lane, pl.ds(512 * lane, 512)
            self.left, self.right = pl.ds(512 * lane, 256), pl.ds(512 * lane + 256, 256)

            def term(number, ez, cols, device):
                return remote(
                    part_out.at[e_rows(ez), cols], land_z.at[lane, number], e_send.at[lane], e_recv.at[lane], number, device
                )

            self.e = [
                term(0, z2, self.left, to_zp),
                term(1, z2, self.right, to_zm),
                term(2, zm, self.left, to_zm),
                term(3, zp, self.right, to_zp),
                term(4, zp, self.left, to_zp),
                term(5, zm, self.right, to_zm),
                remote(
                    part_out.at[aligned(160 * z + 80 * (1 - xhi), 80, 80), self.cols],
                    land_h.at[lane], e_send.at[lane], e_recv.at[lane], 6, to_xhi,
                ),
            ]

        def matmul(self):
            if self.lane == 0:
                loads["basis_out"].wait()
                d[8].wait_recv()
                d[9].wait_recv()

            @pl.loop(0, 2)
            def _(n):
                rows = aligned(320 * n, 320, 320)
                part_out[rows, self.cols] = jnp.dot(
                    g_buf[aligned(640 * core + 320 * n, 320, 320), :], bo_buf[:, self.cols], preferred_element_type=F32
                ) + jnp.dot(g_twin[rows, :], bo_twin[:, self.cols], preferred_element_type=F32)

            for copy in self.e[:4]:
                copy.start()

        def second_a(self):
            self.e[0].wait_recv()
            part_out[e_rows(zp), self.left] += land_z[self.lane, 0]
            self.e[4].start()

        def second_b(self):
            self.e[1].wait_recv()
            part_out[e_rows(zm), self.right] += land_z[self.lane, 1]
            self.e[5].start()

        def total(self):
            for copy in self.e[2:6]:
                copy.wait_recv()
            part_out[e_rows(z), self.left] += land_z[self.lane, 4] + land_z[self.lane, 2]
            part_out[e_rows(z), self.right] += land_z[self.lane, 5] + land_z[self.lane, 3]
            self.e[6].start()

        def finish(self):
            self.e[6].wait_recv()
            rot_out[aligned(640 * core + 160 * z + 80 * xhi, 80, 80), self.cols] = (
                part_out[aligned(160 * z + 80 * xhi, 80, 80), self.cols] + land_h[self.lane]
            ).astype(BF16)
            gather_out[self.lane].start(1, 2, 3, 0)

    lanes = [Lane(0), Lane(1)]
    for lane in lanes:
        ops["outmm%d" % lane.lane] = lane.matmul
        ops["outa%d" % lane.lane] = lane.second_a
        ops["outb%d" % lane.lane] = lane.second_b
        ops["outsum%d" % lane.lane] = lane.total
        ops["outfin%d" % lane.lane] = lane.finish

    def out_done():
        for gather in gather_out:
            gather.wait(0, 4, 7, 9, 10, 11, 13, 14)

    ops["Fdone"] = out_done

    class Unit:
        def __init__(self, u):
            self.u, self.slot = u, u % SLOTS
            if u < 4:
                block_z, block_x = (z, z, zm, zp)[u], (xhi, 1 - xhi, xhi, xhi)[u]
                self.start = 160 * (2 * block_z + block_x)
                self.need = ((0,), (4,), (7,), (9,))[u]
            elif u < 6:
                self.starts = 160 * (2 * zm + 1 - xhi), 160 * (2 * zp + 1 - xhi)
                self.need = (10, 11)
            else:
                self.start = 320 * z2
                self.need = (13, 14)
            self.half = u % 2
            big, small = pl.ds(0, 48), pl.ds(48, 32)
            self.h = (big, small)
            if u % 2 == 0:
                self.up, self.down, to_up, to_down = yp, ym, to_yp, to_ym
                onward_a, onward_b = (48, 32), (0, 48)
            else:
                self.up, self.down, to_up, to_down = ym, yp, to_ym, to_yp
                onward_a, onward_b = (0, 48), (48, 32)

            def term(number, owner, rows, where, device):
                return remote(
                    send.at[u, owner, rows], land.at[u, where, rows], u_send.at[u], u_recv.at[u], number, device
                )

            def spread(number, owner, device, offset=0, count=80, piece=0):
                block = rot_in.at[self.place(owner, offset, count, piece)]
                return remote(block, block, u_send.at[u], u_recv.at[u], number, device)

            self.copies = [
                term(0, y2, big, 0, to_up),
                term(1, y2, small, 0, to_down),
                term(2, self.down, big, 1, to_down),
                term(3, self.up, small, 1, to_up),
                term(4, self.up, big, 2, to_up),
                term(5, self.down, small, 2, to_down),
                remote(send.at[u, y], land.at[u, 3], u_send.at[u], u_recv.at[u], 6, to_xlo),
            ]
            self.pieces = 2 if u in (5, 7) else 1
            for piece in range(self.pieces):
                number = 7 + 4 * piece
                self.copies += [
                    spread(number, y, to_yp, piece=piece),
                    spread(number + 1, y, to_ym, piece=piece),
                    spread(number + 2, ym, to_yp, *onward_a, piece=piece),
                    spread(number + 3, yp, to_ym, *onward_b, piece=piece),
                ]

        def place(self, owner, offset=0, count=80, piece=None):
            if self.u < 4:
                rows = aligned(self.start + 80 * (owner // 2) + offset, 16, count)
                return rows, aligned(HALF * lax.rem(owner, 2), 128, HALF)
            if self.u < 6:
                start = self.starts[0] + (owner // 2) * (self.starts[1] - self.starts[0]) + 80 * lax.rem(owner, 2)
            else:
                start = self.start + 80 * owner
            rows = aligned(start + offset, 16, count)
            if self.half == 0:
                return rows, pl.ds(0, HALF)
            return rows, (pl.ds(HALF, HALF), pl.ds(HALF, 384), pl.ds(HALF + 384, 512))[0 if piece is None else 1 + piece]

        def matmul(self):
            if self.u == 0:
                loads["act"].wait()
            gather_a.wait(*[number for number in self.need if number not in arrived])
            arrived.update(self.need)
            if self.u < 4:
                rows = aligned(self.start, 160, 160)

                def columns(n):
                    block = jnp.dot(
                        a_buf[rows, :], b_buf[:, aligned(HALF * n, HALF, HALF)], preferred_element_type=F32
                    )
                    for half in range(2):
                        piece = block[80 * half:80 * half + 80]
                        part[self.slot, 2 * half + n] = piece
                        send[self.u, 2 * half + n] = piece.astype(BF16)

                if self.u == 0:
                    loads["basis_in_0"].wait()
                    columns(0)
                    loads["basis_in_1"].wait()
                    columns(1)
                    loads["eigen"].start()
                else:
                    pl.loop(0, 2)(columns)
            else:
                cols = slice(HALF * self.half, HALF * self.half + HALF)
                sets = [(start, 160) for start in self.starts] if self.u < 6 else [(self.start, 320)]
                owner = 0
                for start, count in sets:
                    block = jnp.dot(a_buf[aligned(start, 160, count), :], b_buf[:, cols], preferred_element_type=F32)
                    for first in range(0, count, 80):
                        piece = block[first:first + 80]
                        part[self.slot, owner] = piece
                        send[self.u, owner] = piece.astype(BF16)
                        owner += 1
            for copy in self.copies[:4]:
                copy.start()

        def second(self, number):
            owner, rows = ((self.up, self.h[0]), (self.down, self.h[1]))[number]
            self.copies[number].wait_recv()
            send[self.u, owner, rows] = (
                part[self.slot, owner, rows] + land[self.u, 0, rows].astype(F32)
            ).astype(BF16)
            self.copies[4 + number].start()

        def third(self):
            for number in (2, 3, 4, 5):
                self.copies[number].wait_recv()
            total = part[self.slot, y] + (land[self.u, 1].astype(F32) + land[self.u, 2].astype(F32))
            part[self.slot, y] = total
            send[self.u, y] = total.astype(BF16)
            self.copies[6].start()

        def fourth(self):
            self.copies[6].wait_recv()
            rot_in[self.place(y)] = (part[self.slot, y] + land[self.u, 3].astype(F32)).astype(BF16)
            self.give(0)

        def give(self, piece):
            self.copies[7 + 4 * piece].start()
            self.copies[8 + 4 * piece].start()

        def spread_on(self, piece, number):
            self.copies[7 + 4 * piece + number].wait_recv()
            self.copies[9 + 4 * piece + number].start()

        def last(self, piece):
            self.copies[9 + 4 * piece].wait_recv()
            self.copies[10 + 4 * piece].wait_recv()

    arrived = set()
    units = [Unit(u) for u in range(8)]
    for u, unit in enumerate(units):
        ops["mm%d" % u] = unit.matmul
        ops["sa%d" % u] = functools.partial(unit.second, 0)
        ops["sb%d" % u] = functools.partial(unit.second, 1)
        ops["th%d" % u] = unit.third
        ops["fo%d" % u] = unit.fourth
        for piece in range(unit.pieces):
            ops["fg"[piece] + "a%d" % u] = functools.partial(unit.spread_on, piece, 0)
            ops["fg"[piece] + "b%d" % u] = functools.partial(unit.spread_on, piece, 1)
            ops["lk"[piece] + "a%d" % u] = functools.partial(unit.last, piece)
        if unit.pieces == 2:
            ops["go%d" % u] = functools.partial(unit.give, 1)

    def reciprocal():
        loads["eigen"].wait()

        @pl.loop(0, 16)
        def _(n):
            rows = aligned(64 * n, 64, 64)
            eig[rows, :] = 1.0 / eig[rows, :]

    def prepare():
        gather_a.finish()

        @pl.loop(0, 4)
        def _(n):
            rows = aligned(256 * n, 256, 256)
            turned = rot_out[:, rows].astype(F32).T
            for p, (first, last, at) in enumerate(WINDOWS):
                kept = jnp.where(ids[0:1, first:last] == p, turned[:, first:last], 0.0)
                a_buf[rows, at:at + last - first] = kept.astype(BF16)
            a_buf[rows, QUERY_AT:QUERY_AT + 256] = turned[:, 1024:1280].astype(BF16)

        acc[...] = jnp.zeros_like(acc)

    def final(chunks):
        query = a_buf[0:1024, QUERY_AT:QUERY_AT + 256].astype(F32)
        for chunk in chunks:
            cols = slice(256 * chunk, 256 * chunk + 256)
            inverse = eig[:, cols]
            scaled = []
            for first, last, at in WINDOWS:
                pair_block = jnp.dot(
                    a_buf[0:1024, at:at + last - first], rot_in[first:last, cols], preferred_element_type=F32
                )
                scaled.append((pair_block * inverse).astype(BF16))
            mapped = lax.dot_general(
                jnp.concatenate(scaled, axis=0),
                rot_in[1024:1280, cols],
                (((1,), (1,)), ((), ())),
                preferred_element_type=F32,
            )
            for p in range(PAIRS):
                product = mapped[1024 * p:1024 * p + 1024] * query
                acc[8 * p:8 * p + 8, :] += jnp.sum(product.reshape(128, 8, 256), axis=0)

    ops.update(rcp=reciprocal, prep=prepare)
    for number, chunks in enumerate(((0, 1, 2), (3, 4), (5, 6))):
        ops["fin%d" % number] = functools.partial(final, chunks)

    gather_a.start(2, 3, 0)
    d[0].start()
    d[1].start()
    d[9].start()
    for name in ("act", "basis_in_0", "basis_in_1", "grad", "basis_out"):
        loads[name].start()
    for names in ORDER:
        for name in names:
            ops[name]()

    token = lax.broadcasted_iota(jnp.int32, (256, 128), 0)
    query = lax.broadcasted_iota(jnp.int32, (256, 128), 1)
    pick = jnp.where(token // QLEN == query, 1.0, 0.0)
    per_token = jnp.sum(acc[...].reshape(PAIRS, 8, 256), axis=1)
    red_row[row] = jnp.zeros((8, 128), F32)
    red_row[row, :PAIRS] = jnp.dot(per_token, pick, precision=lax.Precision.HIGHEST, preferred_element_type=F32)

    def everyone(red, position, mates, sends, recvs):
        copies = []
        for k, mate in enumerate(mates):
            copies.append(remote(red.at[position], red.at[position], sends, recvs, k, mate))
        for copy in copies:
            copy.start()
        for copy in copies:
            copy.wait_recv()
        return copies

    row_copies = everyone(red_row, row, row_mates, r_send, r_recv)
    red_col[col] = jnp.sum(red_row[...], axis=0)
    col_copies = everyone(red_col, col, col_mates, c_send, c_recv)
    scores[...] = jnp.sum(red_col[...], axis=0)[:PAIRS, :64]

    for gather in gather_out:
        gather.finish()
    for copy in d + lanes[0].e + lanes[1].e + row_copies + col_copies:
        copy.wait_send()
    for unit in units:
        for copy in unit.copies:
            copy.wait_send()


def on_device(activations, gradients, basis_in, basis_out, eigen_damped, pair_ids):
    anywhere = pl.BlockSpec(memory_space=pl.ANY)
    vmem = pl.BlockSpec(memory_space=pltpu.VMEM)
    dma = pltpu.SemaphoreType.DMA
    return pl.pallas_call(
        kernel,
        out_shape=jax.ShapeDtypeStruct((PAIRS, 64), F32),
        in_specs=[anywhere] * 5 + [vmem],
        out_specs=vmem,
        scratch_shapes=[
            pltpu.VMEM((1280, 3584), BF16),
            pltpu.VMEM((3584, 1792), BF16),
            pltpu.VMEM((SLOTS, 4, 80, HALF), F32),
            pltpu.VMEM((8, 4, 80, HALF), BF16),
            pltpu.VMEM((8, 4, 80, HALF), BF16),
            pltpu.VMEM((1280, 1792), BF16),
            pltpu.VMEM((1280, 512), BF16),
            pltpu.VMEM((640, 512), BF16),
            pltpu.VMEM((512, 1024), BF16),
            pltpu.VMEM((512, 1024), BF16),
            pltpu.VMEM((640, 1024), F32),
            pltpu.VMEM((2, 6, 160, 256), F32),
            pltpu.VMEM((2, 80, 512), F32),
            pltpu.VMEM((1280, 1024), BF16),
            pltpu.VMEM((1024, 1792), F32),
            pltpu.VMEM((8 * PAIRS, 256), F32),
            pltpu.VMEM((8, 8, 128), F32),
            pltpu.VMEM((16, 8, 128), F32),
            dma((15,)), dma((15,)),
            dma((10,)), dma((10,)),
            dma((2, 7)), dma((2, 7)),
            dma((2, 15)), dma((2, 15)),
            dma((8, 15)), dma((8, 15)),
            dma((7,)), dma((7,)),
            dma((15,)), dma((15,)),
            dma((6,)),
        ],
        compiler_params=pltpu.CompilerParams(
            collective_id=0, has_side_effects=True, vmem_limit_bytes=63 * 2**20
        ),
        cost_estimate=pl.CostEstimate(flops=28 * 10**9, bytes_accessed=22 * 10**6, transcendentals=0),
    )(activations, gradients, basis_in, basis_out, eigen_damped, pair_ids.reshape(1, 1024))


def solution(mesh):
    return jax.shard_map(
        on_device,
        mesh=mesh,
        in_specs=(
            P("col", "row"),
            P("row", "col"),
            P("row", "col"),
            P("col", "row"),
            P("row", "col"),
            P(),
        ),
        out_specs=P(),
        check_vma=False,
    )
```

```python
import functools

import jax
import jax.numpy as jnp
from jax import lax
from jax.experimental import pallas as pl
from jax.experimental.pallas import tpu as pltpu
from jax.sharding import PartitionSpec as P

PAIRS = 4
QLEN = 4
WINDOWS = ((0, 384, 0), (0, 768, 384), (256, 1024, 1152), (640, 1024, 1920))
QUERY_AT = 2304
HALF = 896
SLOTS = 5
MESH = pl.DeviceIdType.MESH
BF16 = jnp.bfloat16
F32 = jnp.float32


def aligned(start, multiple, size):
    return pl.ds(pl.multiple_of(start, multiple), size)


class Place:
    def __init__(self):
        row, col = lax.axis_index("row"), lax.axis_index("col")
        self.xlo, self.y = row // 4, lax.rem(row, 4)
        self.z, self.xhi, self.core = col // 4, lax.rem(col // 2, 2), lax.rem(col, 2)

    def at(self, xlo=None, y=None, z=None, xhi=None, core=None):
        xlo = self.xlo if xlo is None else xlo
        y = self.y if y is None else y
        z = self.z if z is None else z
        xhi = self.xhi if xhi is None else xhi
        core = self.core if core is None else core
        return (xlo * 4 + y, z * 4 + xhi * 2 + core)


def remote(src, dst, sends, recvs, number, device):
    return pltpu.make_async_remote_copy(
        src_ref=src,
        dst_ref=dst,
        send_sem=sends.at[number],
        recv_sem=recvs.at[number],
        device_id=device,
        device_id_type=MESH,
    )


class Gather:
    def __init__(self, place, buf, slot, sends, recvs, first=None):
        zp, zm, z2 = (lax.rem(place.z + k, 4) for k in (1, 3, 2))
        xhi, other = place.xhi, 1 - place.xhi
        core, twin = place.core, 1 - place.core
        to_core, to_xhi = place.at(core=twin), place.at(xhi=other)
        to_zp, to_zm = place.at(z=zp), place.at(z=zm)
        z = place.z
        plan = [
            (z, xhi, to_core), (z, xhi, to_xhi), (z, xhi, to_zp), (z, xhi, to_zm),
            (z, other, to_core), (z, other, to_zp), (z, other, to_zm),
            (zm, xhi, to_core), (zm, xhi, to_zp), (zp, xhi, to_core),
            (zm, other, to_core), (zp, other, to_core), (zp, other, to_zm),
            (z2, xhi, to_core), (z2, other, to_core),
        ]
        self.copies = []
        for number, (from_z, from_x, device) in enumerate(plan):
            block = buf.at[slot(from_z, from_x, core)]
            src = first if number < 4 and first is not None else block
            self.copies.append(remote(src, block, sends, recvs, number, device))

    def start(self, *numbers):
        for number in numbers:
            self.copies[number].start()

    def wait(self, *numbers):
        for number in numbers:
            self.copies[number].wait_recv()

    def finish(self):
        for copy in self.copies:
            copy.wait_send()


ORDER = (
    ("Ax", "mm0", "Da", "Dc2", "sa0", "sb0", "A3", "A1", "th0", "Dc4", "Db", "mm3", "fo0", "A2", "mm1", "Dc7"),
    ("mm2", "A5", "sb3", "A6", "sa3", "Dc6", "sa1", "rcp", "sb1", "mm4", "sa2", "Dx", "sb2", "mm5", "outmm0"),
    ("sb4", "A8", "th1", "A12", "sa4", "sb5", "sa5", "th3", "th2", "outb0", "fo1", "outa0", "mm6", "th5", "fo3"),
    ("outmm1", "fo2", "fb0", "outsum0", "sb6", "fa0", "outb1", "sa6", "th4", "outa1", "mm7", "outfin0", "fb2"),
    ("fo4", "fb1", "fa2", "fa1", "fb3", "outsum1", "sb7", "th6", "F1", "fa3", "F3", "sa7", "F6", "la0", "outfin1"),
    ("fa4", "fb4", "F2", "fo5", "la1", "fo6", "go5", "H1", "F12", "th7", "H2", "H6", "H5", "fo7", "la3", "H3"),
    ("fa6", "fb6", "la2", "F8", "fb5", "H12", "F5", "go7", "H8", "Fdone", "fa5", "gb5", "la4", "prep", "ga5"),
    ("fb7", "fa7", "la6", "fin0", "ga7", "la5", "la7", "gb7", "ka5", "fin1", "ka7", "fin2"),
)


def kernel(
    act, grad, basis_in, basis_out, eigen, ids, scores,
    a_buf, b_buf, part, send, land, rot_in,
    g_buf, g_twin, bo_buf, bo_twin, part_out, land_z, land_h, rot_out,
    eig, acc, red_row, red_col,
    a_send, a_recv, d_send, d_recv, e_send, e_recv, f_send, f_recv, u_send, u_recv,
    r_send, r_recv, c_send, c_recv, local,
):
    me = Place()
    row, col = lax.axis_index("row"), lax.axis_index("col")
    xlo, y, z, xhi, core = me.xlo, me.y, me.z, me.xhi, me.core
    yp, ym, y2 = (lax.rem(y + k, 4) for k in (1, 3, 2))
    zp, zm, z2 = (lax.rem(z + k, 4) for k in (1, 3, 2))
    to_yp, to_ym = me.at(y=yp), me.at(y=ym)
    to_zp, to_zm = me.at(z=zp), me.at(z=zm)
    to_xlo, to_xhi, to_core = me.at(xlo=1 - xlo), me.at(xhi=1 - xhi), me.at(core=1 - core)
    row_mates = [(lax.rem(row + k, 8), col) for k in range(1, 8)]
    col_mates = [(row, lax.rem(col + k, 16)) for k in range(1, 16)]

    parity = lax.rem(y, 2)
    first_half, second_half = aligned(HALF * parity, HALF, HALF), aligned(HALF * (1 - parity), HALF, HALF)
    loads = {
        "act": pltpu.make_async_copy(act, a_buf.at[aligned(80 * (4 * z + 2 * xhi + core), 80, 80)], local.at[0]),
        "grad": pltpu.make_async_copy(grad, g_buf.at[aligned(160 * (4 * xlo + y), 160, 160)], local.at[1]),
        "basis_in_0": pltpu.make_async_copy(basis_in.at[:, first_half], b_buf.at[:, first_half], local.at[2]),
        "basis_in_1": pltpu.make_async_copy(basis_in.at[:, second_half], b_buf.at[:, second_half], local.at[5]),
        "basis_out": pltpu.make_async_copy(basis_out, bo_buf, local.at[3]),
        "eigen": pltpu.make_async_copy(eigen, eig, local.at[4]),
    }
    barrier = pltpu.get_barrier_semaphore()
    friends = (to_yp, to_ym, to_zp, to_zm, to_xlo, to_xhi, to_core)
    for friend in friends:
        pl.semaphore_signal(barrier, inc=1, device_id=friend, device_id_type=MESH)
    pl.semaphore_wait(barrier, len(friends))

    ops = {}

    gather_a = Gather(
        me, a_buf, lambda gz, gx, gc: aligned(80 * (4 * gz + 2 * gx + gc), 80, 80), a_send, a_recv, act
    )
    gather_out = [
        Gather(
            me, rot_out.at[:, pl.ds(512 * lane, 512)],
            lambda gz, gx, gc: aligned(640 * gc + 160 * gz + 80 * gx, 80, 80), f_send.at[lane], f_recv.at[lane],
        )
        for lane in range(2)
    ]
    onward = {1: (5, 6, 4), 2: (8, 7), 3: (9,), 5: (10,), 6: (12, 11), 8: (13,), 12: (14,)}

    def forward(gather, number):
        gather.wait(number)
        gather.start(*onward[number])

    for number in onward:
        ops["A%d" % number] = functools.partial(forward, gather_a, number)
        ops["F%d" % number] = functools.partial(forward, gather_out[0], number)
        ops["H%d" % number] = functools.partial(forward, gather_out[1], number)
    ops["Ax"] = functools.partial(gather_a.start, 1)

    def g_slot(gy, gx):
        return aligned(160 * (4 * gx + gy), 160, 160)

    def d_copy(number, rows, device, src=None):
        block = g_buf.at[rows]
        return remote(block if src is None else src, block, d_send, d_recv, number, device)

    d = [
        d_copy(0, g_slot(y, xlo), to_yp, grad),
        d_copy(1, g_slot(y, xlo), to_ym, grad),
        d_copy(2, g_slot(y, xlo), to_xlo, grad),
        d_copy(3, aligned(160 * (4 * xlo + ym), 80, 80), to_yp),
        d_copy(4, g_slot(ym, xlo), to_xlo),
        d_copy(5, aligned(160 * (4 * xlo + yp) + 80, 80, 80), to_ym),
        d_copy(6, g_slot(yp, xlo), to_xlo),
        d_copy(7, g_slot(y2, xlo), to_xlo),
        remote(g_buf.at[aligned(640 * (1 - core), 640, 640)], g_twin, d_send, d_recv, 8, to_core),
        remote(basis_out, bo_twin, d_send, d_recv, 9, to_core),
    ]

    def gradients_a():
        d[0].wait_recv()
        d[3].start()

    def gradients_b():
        d[1].wait_recv()
        d[5].start()

    def gradients_across(number):
        if number == 7:
            d[3].wait_recv()
            d[5].wait_recv()
        d[number].start()

    def gradients_x():
        for number in (2, 4, 6, 7):
            d[number].wait_recv()
        loads["grad"].wait()
        d[8].start()

    ops.update(Da=gradients_a, Db=gradients_b, Dx=gradients_x)
    for number in (2, 4, 6, 7):
        ops["Dc%d" % number] = functools.partial(gradients_across, number)

    def e_rows(ez):
        return aligned(160 * ez, 160, 160)

    class Lane:
        def __init__(self, lane):
            self.lane, self.cols = lane, pl.ds(512 * lane, 512)
            self.left, self.right = pl.ds(512 * lane, 256), pl.ds(512 * lane + 256, 256)

            def term(number, ez, cols, device):
                return remote(
                    part_out.at[e_rows(ez), cols], land_z.at[lane, number], e_send.at[lane], e_recv.at[lane], number, device
                )

            self.e = [
                term(0, z2, self.left, to_zp),
                term(1, z2, self.right, to_zm),
                term(2, zm, self.left, to_zm),
                term(3, zp, self.right, to_zp),
                term(4, zp, self.left, to_zp),
                term(5, zm, self.right, to_zm),
                remote(
                    part_out.at[aligned(160 * z + 80 * (1 - xhi), 80, 80), self.cols],
                    land_h.at[lane], e_send.at[lane], e_recv.at[lane], 6, to_xhi,
                ),
            ]

        def matmul(self):
            if self.lane == 0:
                loads["basis_out"].wait()
                d[8].wait_recv()
                d[9].wait_recv()

            @pl.loop(0, 2)
            def _(n):
                rows = aligned(320 * n, 320, 320)
                part_out[rows, self.cols] = jnp.dot(
                    g_buf[aligned(640 * core + 320 * n, 320, 320), :], bo_buf[:, self.cols], preferred_element_type=F32
                ) + jnp.dot(g_twin[rows, :], bo_twin[:, self.cols], preferred_element_type=F32)

            for copy in self.e[:4]:
                copy.start()

        def second_a(self):
            self.e[0].wait_recv()
            part_out[e_rows(zp), self.left] += land_z[self.lane, 0]
            self.e[4].start()

        def second_b(self):
            self.e[1].wait_recv()
            part_out[e_rows(zm), self.right] += land_z[self.lane, 1]
            self.e[5].start()

        def total(self):
            for copy in self.e[2:6]:
                copy.wait_recv()
            part_out[e_rows(z), self.left] += land_z[self.lane, 4] + land_z[self.lane, 2]
            part_out[e_rows(z), self.right] += land_z[self.lane, 5] + land_z[self.lane, 3]
            self.e[6].start()

        def finish(self):
            self.e[6].wait_recv()
            rot_out[aligned(640 * core + 160 * z + 80 * xhi, 80, 80), self.cols] = (
                part_out[aligned(160 * z + 80 * xhi, 80, 80), self.cols] + land_h[self.lane]
            ).astype(BF16)
            gather_out[self.lane].start(1, 2, 3, 0)

    lanes = [Lane(0), Lane(1)]
    for lane in lanes:
        ops["outmm%d" % lane.lane] = lane.matmul
        ops["outa%d" % lane.lane] = lane.second_a
        ops["outb%d" % lane.lane] = lane.second_b
        ops["outsum%d" % lane.lane] = lane.total
        ops["outfin%d" % lane.lane] = lane.finish

    def out_done():
        for gather in gather_out:
            gather.wait(0, 4, 7, 9, 10, 11, 13, 14)

    ops["Fdone"] = out_done

    class Unit:
        def __init__(self, u):
            self.u, self.slot = u, u % SLOTS
            if u < 4:
                block_z, block_x = (z, z, zm, zp)[u], (xhi, 1 - xhi, xhi, xhi)[u]
                self.start = 160 * (2 * block_z + block_x)
                self.need = ((0,), (4,), (7,), (9,))[u]
            elif u < 6:
                self.starts = 160 * (2 * zm + 1 - xhi), 160 * (2 * zp + 1 - xhi)
                self.need = (10, 11)
            else:
                self.start = 320 * z2
                self.need = (13, 14)
            self.half = u % 2
            big, small = pl.ds(0, 48), pl.ds(48, 32)
            self.h = (big, small)
            if u % 2 == 0:
                self.up, self.down, to_up, to_down = yp, ym, to_yp, to_ym
                onward_a, onward_b = (48, 32), (0, 48)
            else:
                self.up, self.down, to_up, to_down = ym, yp, to_ym, to_yp
                onward_a, onward_b = (0, 48), (48, 32)

            def term(number, owner, rows, where, device):
                return remote(
                    send.at[u, owner, rows], land.at[u, where, rows], u_send.at[u], u_recv.at[u], number, device
                )

            def spread(number, owner, device, offset=0, count=80, piece=0):
                block = rot_in.at[self.place(owner, offset, count, piece)]
                return remote(block, block, u_send.at[u], u_recv.at[u], number, device)

            self.copies = [
                term(0, y2, big, 0, to_up),
                term(1, y2, small, 0, to_down),
                term(2, self.down, big, 1, to_down),
                term(3, self.up, small, 1, to_up),
                term(4, self.up, big, 2, to_up),
                term(5, self.down, small, 2, to_down),
                remote(send.at[u, y], land.at[u, 3], u_send.at[u], u_recv.at[u], 6, to_xlo),
            ]
            self.pieces = 2 if u in (5, 7) else 1
            for piece in range(self.pieces):
                number = 7 + 4 * piece
                self.copies += [
                    spread(number, y, to_yp, piece=piece),
                    spread(number + 1, y, to_ym, piece=piece),
                    spread(number + 2, ym, to_yp, *onward_a, piece=piece),
                    spread(number + 3, yp, to_ym, *onward_b, piece=piece),
                ]

        def place(self, owner, offset=0, count=80, piece=None):
            if self.u < 4:
                rows = aligned(self.start + 80 * (owner // 2) + offset, 16, count)
                return rows, aligned(HALF * lax.rem(owner, 2), 128, HALF)
            if self.u < 6:
                start = self.starts[0] + (owner // 2) * (self.starts[1] - self.starts[0]) + 80 * lax.rem(owner, 2)
            else:
                start = self.start + 80 * owner
            rows = aligned(start + offset, 16, count)
            if self.half == 0:
                return rows, pl.ds(0, HALF)
            return rows, (pl.ds(HALF, HALF), pl.ds(HALF, 384), pl.ds(HALF + 384, 512))[0 if piece is None else 1 + piece]

        def matmul(self):
            if self.u == 0:
                loads["act"].wait()
            gather_a.wait(*[number for number in self.need if number not in arrived])
            arrived.update(self.need)
            if self.u < 4:
                rows = aligned(self.start, 160, 160)

                def columns(n):
                    block = jnp.dot(
                        a_buf[rows, :], b_buf[:, aligned(HALF * n, HALF, HALF)], preferred_element_type=F32
                    )
                    for half in range(2):
                        piece = block[80 * half:80 * half + 80]
                        part[self.slot, 2 * half + n] = piece
                        send[self.u, 2 * half + n] = piece.astype(BF16)

                if self.u == 0:
                    loads["basis_in_0"].wait()
                    columns(parity)
                    self.copies[0].start()
                    self.copies[1].start()
                    loads["basis_in_1"].wait()
                    columns(1 - parity)
                    loads["eigen"].start()
                else:
                    pl.loop(0, 2)(columns)
            else:
                cols = slice(HALF * self.half, HALF * self.half + HALF)
                sets = [(start, 160) for start in self.starts] if self.u < 6 else [(self.start, 320)]
                owner = 0
                for start, count in sets:
                    block = jnp.dot(a_buf[aligned(start, 160, count), :], b_buf[:, cols], preferred_element_type=F32)
                    for first in range(0, count, 80):
                        piece = block[first:first + 80]
                        part[self.slot, owner] = piece
                        send[self.u, owner] = piece.astype(BF16)
                        owner += 1
            for copy in self.copies[2 if self.u == 0 else 0:4]:
                copy.start()

        def second(self, number):
            owner, rows = ((self.up, self.h[0]), (self.down, self.h[1]))[number]
            self.copies[number].wait_recv()
            send[self.u, owner, rows] = (
                part[self.slot, owner, rows] + land[self.u, 0, rows].astype(F32)
            ).astype(BF16)
            self.copies[4 + number].start()

        def third(self):
            for number in (2, 3, 4, 5):
                self.copies[number].wait_recv()
            total = part[self.slot, y] + (land[self.u, 1].astype(F32) + land[self.u, 2].astype(F32))
            part[self.slot, y] = total
            send[self.u, y] = total.astype(BF16)
            self.copies[6].start()

        def fourth(self):
            self.copies[6].wait_recv()
            rot_in[self.place(y)] = (part[self.slot, y] + land[self.u, 3].astype(F32)).astype(BF16)
            self.give(0)

        def give(self, piece):
            self.copies[7 + 4 * piece].start()
            self.copies[8 + 4 * piece].start()

        def spread_on(self, piece, number):
            self.copies[7 + 4 * piece + number].wait_recv()
            self.copies[9 + 4 * piece + number].start()

        def last(self, piece):
            self.copies[9 + 4 * piece].wait_recv()
            self.copies[10 + 4 * piece].wait_recv()

    arrived = set()
    units = [Unit(u) for u in range(8)]
    for u, unit in enumerate(units):
        ops["mm%d" % u] = unit.matmul
        ops["sa%d" % u] = functools.partial(unit.second, 0)
        ops["sb%d" % u] = functools.partial(unit.second, 1)
        ops["th%d" % u] = unit.third
        ops["fo%d" % u] = unit.fourth
        for piece in range(unit.pieces):
            ops["fg"[piece] + "a%d" % u] = functools.partial(unit.spread_on, piece, 0)
            ops["fg"[piece] + "b%d" % u] = functools.partial(unit.spread_on, piece, 1)
            ops["lk"[piece] + "a%d" % u] = functools.partial(unit.last, piece)
        if unit.pieces == 2:
            ops["go%d" % u] = functools.partial(unit.give, 1)

    def reciprocal():
        loads["eigen"].wait()

        @pl.loop(0, 16)
        def _(n):
            rows = aligned(64 * n, 64, 64)
            eig[rows, :] = 1.0 / eig[rows, :]

    def prepare():
        gather_a.finish()

        @pl.loop(0, 4)
        def _(n):
            rows = aligned(256 * n, 256, 256)
            turned = rot_out[:, rows].astype(F32).T
            for p, (first, last, at) in enumerate(WINDOWS):
                kept = jnp.where(ids[0:1, first:last] == p, turned[:, first:last], 0.0)
                a_buf[rows, at:at + last - first] = kept.astype(BF16)
            a_buf[rows, QUERY_AT:QUERY_AT + 256] = turned[:, 1024:1280].astype(BF16)

        acc[...] = jnp.zeros_like(acc)

    def final(chunks):
        query = a_buf[0:1024, QUERY_AT:QUERY_AT + 256].astype(F32)
        for chunk in chunks:
            cols = slice(256 * chunk, 256 * chunk + 256)
            inverse = eig[:, cols]
            scaled = []
            for first, last, at in WINDOWS:
                pair_block = jnp.dot(
                    a_buf[0:1024, at:at + last - first], rot_in[first:last, cols], preferred_element_type=F32
                )
                scaled.append((pair_block * inverse).astype(BF16))
            mapped = lax.dot_general(
                jnp.concatenate(scaled, axis=0),
                rot_in[1024:1280, cols],
                (((1,), (1,)), ((), ())),
                preferred_element_type=F32,
            )
            for p in range(PAIRS):
                product = mapped[1024 * p:1024 * p + 1024] * query
                acc[8 * p:8 * p + 8, :] += jnp.sum(product.reshape(128, 8, 256), axis=0)

    ops.update(rcp=reciprocal, prep=prepare)
    for number, chunks in enumerate(((0, 1, 2), (3, 4), (5, 6))):
        ops["fin%d" % number] = functools.partial(final, chunks)

    gather_a.start(2, 3, 0)
    d[0].start()
    d[1].start()
    d[9].start()
    for name in ("act", "basis_in_0", "basis_in_1", "grad", "basis_out"):
        loads[name].start()
    for names in ORDER:
        for name in names:
            ops[name]()

    token = lax.broadcasted_iota(jnp.int32, (256, 128), 0)
    query = lax.broadcasted_iota(jnp.int32, (256, 128), 1)
    pick = jnp.where(token // QLEN == query, 1.0, 0.0)
    per_token = jnp.sum(acc[...].reshape(PAIRS, 8, 256), axis=1)
    red_row[row] = jnp.zeros((8, 128), F32)
    red_row[row, :PAIRS] = jnp.dot(per_token, pick, precision=lax.Precision.HIGHEST, preferred_element_type=F32)

    def everyone(red, position, mates, sends, recvs):
        copies = []
        for k, mate in enumerate(mates):
            copies.append(remote(red.at[position], red.at[position], sends, recvs, k, mate))
        for copy in copies:
            copy.start()
        for copy in copies:
            copy.wait_recv()
        return copies

    row_copies = everyone(red_row, row, row_mates, r_send, r_recv)
    red_col[col] = jnp.sum(red_row[...], axis=0)
    col_copies = everyone(red_col, col, col_mates, c_send, c_recv)
    scores[...] = jnp.sum(red_col[...], axis=0)[:PAIRS, :64]

    for gather in gather_out:
        gather.finish()
    for copy in d + lanes[0].e + lanes[1].e + row_copies + col_copies:
        copy.wait_send()
    for unit in units:
        for copy in unit.copies:
            copy.wait_send()


def on_device(activations, gradients, basis_in, basis_out, eigen_damped, pair_ids):
    anywhere = pl.BlockSpec(memory_space=pl.ANY)
    vmem = pl.BlockSpec(memory_space=pltpu.VMEM)
    dma = pltpu.SemaphoreType.DMA
    return pl.pallas_call(
        kernel,
        out_shape=jax.ShapeDtypeStruct((PAIRS, 64), F32),
        in_specs=[anywhere] * 5 + [vmem],
        out_specs=vmem,
        scratch_shapes=[
            pltpu.VMEM((1280, 3584), BF16),
            pltpu.VMEM((3584, 1792), BF16),
            pltpu.VMEM((SLOTS, 4, 80, HALF), F32),
            pltpu.VMEM((8, 4, 80, HALF), BF16),
            pltpu.VMEM((8, 4, 80, HALF), BF16),
            pltpu.VMEM((1280, 1792), BF16),
            pltpu.VMEM((1280, 512), BF16),
            pltpu.VMEM((640, 512), BF16),
            pltpu.VMEM((512, 1024), BF16),
            pltpu.VMEM((512, 1024), BF16),
            pltpu.VMEM((640, 1024), F32),
            pltpu.VMEM((2, 6, 160, 256), F32),
            pltpu.VMEM((2, 80, 512), F32),
            pltpu.VMEM((1280, 1024), BF16),
            pltpu.VMEM((1024, 1792), F32),
            pltpu.VMEM((8 * PAIRS, 256), F32),
            pltpu.VMEM((8, 8, 128), F32),
            pltpu.VMEM((16, 8, 128), F32),
            dma((15,)), dma((15,)),
            dma((10,)), dma((10,)),
            dma((2, 7)), dma((2, 7)),
            dma((2, 15)), dma((2, 15)),
            dma((8, 15)), dma((8, 15)),
            dma((7,)), dma((7,)),
            dma((15,)), dma((15,)),
            dma((6,)),
        ],
        compiler_params=pltpu.CompilerParams(
            collective_id=0, has_side_effects=True, vmem_limit_bytes=63 * 2**20
        ),
        cost_estimate=pl.CostEstimate(flops=28 * 10**9, bytes_accessed=22 * 10**6, transcendentals=0),
    )(activations, gradients, basis_in, basis_out, eigen_damped, pair_ids.reshape(1, 1024))


def solution(mesh):
    return jax.shard_map(
        on_device,
        mesh=mesh,
        in_specs=(
            P("col", "row"),
            P("row", "col"),
            P("row", "col"),
            P("col", "row"),
            P("row", "col"),
            P(),
        ),
        out_specs=P(),
        check_vma=False,
    )
```
